256 devices in a mesh: comp: 2 (over core), gx: 8 (over z_hi, x), gy: 16 (over z_lo, y).
Axes of the slice: x: 4, y: 4, z: 8 (z_hi: 2, z_lo: 4; z = z_hi * 4 + z_lo), core: 2. Of those that a mesh axis runs over, the one named last changes fastest.
Arguments:
- cotangent: float32 [2, 8, 16, 320, 1024], P('comp', 'gx', 'gy'), may hold values from -6 to 6
- metric: float32 [2, 8, 16, 64, 1024], P('comp', 'gx', 'gy'), may hold values from 0.3 to 3
- volume_ops: bfloat16 [2, 320, 320], P('comp'), may hold values from -0.3125 to 0.3125
- face_ops: float32 [2, 6, 80, 80], P('comp'), may hold values from -0.625 to 0.625
- land_mask: int32 [8, 16, 256], P('gx', 'gy'), may hold values 0 or 1
- intersection: int32 [16], replicated, may hold values from 0 to 7
Outputs:
- adjoint_state: float32 [2, 8, 16, 320, 1024], P('comp', 'gx', 'gy')
The draws below stay inside these ranges and needn't reach their ends.
All inputs are finite; a program needn't handle non-finite values. No bound on the sum of `land_mask` on one device may be relied on, other than what follows from the above.
Results may differ from the reference program's by a relative error of at most 0.0015.
Values sent between devices are 32-bit elements; how exact they have to be, the bound alone decides.
A program may use at most 64 MiB of HBM per device.

```python
import math
import jax
import jax.numpy as jnp
from jax import lax

CX = 16
CY = 16
LEV = 4
TX = 8
TY = 16
COLS = 256
ELEM = 1024


def set_ends(array, rng, smallest, high):
    shape = array.shape
    spot = [jax.random.randint(jax.random.fold_in(rng, axis), (), 0, shape[axis]) for axis in range(len(shape))]
    array = array.at[tuple(spot)].set(smallest)
    longest = shape.index(max(shape))
    spot[longest] = (spot[longest] + 1) % shape[longest]
    return array.at[tuple(spot)].set(high)


def block_scale(key, dims, split, low, largest):
    def one(position, shards_of):
        draws = jax.random.uniform(jax.random.fold_in(jax.random.fold_in(key, 6), position), (shards_of,), jnp.float32, low / len(split), largest / len(split))
        return jnp.repeat(jnp.exp(draws), dims[position] // shards_of).reshape((-1,) + (1,) * (len(dims) - position - 1))

    loudness = one(*split[0])
    for cut in split[1:]:
        loudness = loudness * one(*cut)
    return loudness


def gaussian(key, extent, spread, bound, shards=(), kind=jnp.bfloat16):
    values = spread * jax.random.normal(key, extent, jnp.float32)
    if shards:
        values = values * block_scale(key, extent, shards, -0.22, 0.18)
    return jnp.clip(values, -bound, bound).astype(kind)


def setup_inputs(seed: int = 0) -> dict:
    keys = jax.random.split(jax.random.key(seed), 7)
    cotangent = gaussian(keys[0], (2, TX, TY, 320, ELEM), 1.0, 6.0, ((0, 2), (1, 8), (2, 16)), jnp.float32)
    metric = jnp.clip(jnp.exp(math.log(3.0) - 2.3025851 * jax.random.uniform(keys[1], (2, TX, TY, 64, ELEM), jnp.float32) ** block_scale(keys[1], (2, TX, TY, 64, ELEM), ((0, 2), (1, 8), (2, 16)), -0.2, 0.2)), 0.3, 3.0)
    volume_ops = gaussian(keys[2], (2, 320, 320), 320 ** -0.5, 0.3125, ((0, 2),))
    face_ops = gaussian(keys[3], (2, 6, 80, 80), 80 ** -0.5, 0.625, ((0, 2),), jnp.float32)
    land_mask = set_ends((jax.random.randint(keys[4], (TX, TY, COLS), 0, 10) < 7).astype(jnp.int32), jax.random.fold_in(keys[4], 1), 0, 1)
    intersection = set_ends(jax.random.randint(keys[5], (TY,), 0, TX), jax.random.fold_in(keys[5], 1), 0, TX - 1).astype(jnp.int32)
    return {"cotangent": cotangent, "metric": metric, "volume_ops": volume_ops, "face_ops": face_ops, "land_mask": land_mask, "intersection": intersection}


DT_STEP = 0.4
FACE_SLOTS = ((-6, 0), (-6, 3), (-5, 0), (-5, 3), (-4, 0), (-4, 3))


def face_traces(field):
    nodal = field.reshape(field.shape[:-2] + (5, 4, 4, 4, LEV, CX, CY))
    return [jnp.take(nodal, node_pos, axis=node_axis) for node_axis, node_pos in FACE_SLOTS]


def across_faces(own_faces, west_rim, east_rim, south_rim, north_rim, below_rim, above_rim):
    x_low, x_high, y_low, y_high, z_low, z_high = own_faces
    return [
        jnp.concatenate([west_rim[..., None, :], x_high[..., :-1, :]], axis=-2),
        jnp.concatenate([x_low[..., 1:, :], east_rim[..., None, :]], axis=-2),
        jnp.concatenate([south_rim[..., None], y_high[..., :-1]], axis=-1),
        jnp.concatenate([y_low[..., 1:], north_rim[..., None]], axis=-1),
        jnp.concatenate([below_rim[..., None, :, :], z_high[..., :-1, :, :]], axis=-3),
        jnp.concatenate([z_low[..., 1:, :, :], above_rim[..., None, :, :]], axis=-3),
    ]


def assemble(own_faces, neighbours, weights, volume_term, face_ops):
    leading = volume_term.shape[:-2]
    elems = volume_term.shape[-1]
    result = volume_term.reshape(leading + (5, 64, elems)) * weights[..., None, :, :]
    result = result.reshape(leading + (5, 4, 4, 4, elems))
    for face_no in range(6):
        node_axis, node_pos = FACE_SLOTS[face_no]
        jump_term = (neighbours[face_no] - own_faces[face_no]).reshape(leading + (80, elems))
        lifted = jnp.einsum("ij,...je->...ie", face_ops[face_no], jump_term, precision=lax.Precision.HIGHEST)
        lifted = jnp.expand_dims(lifted.reshape(leading + (5, 4, 4, elems)), node_axis + 2)
        widths = [(0, 0)] * result.ndim
        widths[result.ndim + node_axis + 2] = (node_pos, 3 - node_pos)
        result = result + jnp.pad(lifted, widths)
    return result.reshape(leading + (320, elems))


def column_mask(field, mask_f):
    leading = field.shape[:-2]
    shaped = field.reshape(leading + (320, LEV, CX * CY)) * mask_f[..., None, None, :]
    return shaped.reshape(field.shape)


def apply_adjoint(state, metric, volume_ops, face_ops, mask_f, intersection):
    tiles_x = state.shape[1]
    tiles_y = state.shape[2]
    faces_all = [face_traces(state[0]), face_traces(state[1])]
    row_ids = jnp.arange(tiles_x, dtype=jnp.int32)[:, None]
    col_ids = jnp.arange(tiles_y, dtype=jnp.int32)[None, :]
    above_src = (row_ids + intersection[None, :]) % tiles_x
    below_src = (row_ids - intersection[None, :] + tiles_x) % tiles_x
    ocean_top = faces_all[1][5][..., LEV - 1, :, :]
    air_bottom = faces_all[0][4][..., 0, :, :]
    to_air = ocean_top[above_src, col_ids]
    to_ocean = air_bottom[below_src, col_ids]
    zeros_rim = jnp.zeros_like(air_bottom)
    results = []
    for section in range(2):
        own_faces = faces_all[section]
        west = jnp.roll(own_faces[1][..., CX - 1, :], 1, axis=0)
        east = jnp.roll(own_faces[0][..., 0, :], -1, axis=0)
        south_src = own_faces[3][..., CY - 1]
        south = jnp.concatenate([jnp.zeros_like(south_src[:, :1]), south_src[:, :-1]], axis=1)
        north_src = own_faces[2][..., 0]
        north = jnp.concatenate([north_src[:, 1:], jnp.zeros_like(north_src[:, :1])], axis=1)
        below = to_air if section == 0 else zeros_rim
        above = zeros_rim if section == 0 else to_ocean
        rounded = lax.optimization_barrier(state[section].astype(jnp.bfloat16)).astype(jnp.float32)
        volume_term = jnp.einsum("ij,xyje->xyie", volume_ops[section].astype(jnp.float32), rounded,
                                 precision=lax.Precision.HIGHEST)
        neighbours = across_faces(own_faces, west, east, south, north, below, above)
        result = assemble(own_faces, neighbours, metric[section], volume_term, face_ops[section])
        if section == 1:
            result = column_mask(result, mask_f)
        results.append(result)
    return jnp.stack(results)


def reference(cotangent, metric, volume_ops, face_ops, land_mask, intersection):
    mask_f = land_mask.astype(jnp.float32)
    start = jnp.stack([cotangent[0], column_mask(cotangent[1], mask_f)])
    half_state = 0.5 * start
    segment_one = half_state + DT_STEP * apply_adjoint(half_state, metric, volume_ops, face_ops, mask_f, intersection)
    return 0.5 * start + segment_one + DT_STEP * apply_adjoint(segment_one, metric, volume_ops, face_ops, mask_f, intersection)
```

```python
import functools

import jax
import jax.numpy as jnp
from jax import lax
from jax.experimental import pallas as pl
from jax.experimental.pallas import tpu as pltpu
from jax.sharding import PartitionSpec as P

MESH = pl.DeviceIdType.MESH
F32 = jnp.float32
BF16 = jnp.bfloat16
ROWS = 320
COLS = 256
LEV = 4
FACE = 80
SLOT = 256
STEP = 0.4


def iota(shape, axis):
    return lax.broadcasted_iota(jnp.int32, shape, axis)


def split3(x):
    high = x.astype(BF16)
    low = (x - high.astype(F32)).astype(BF16)
    return jnp.concatenate([high, low, high, jnp.zeros((16, x.shape[1]), BF16)], axis=0)


def a_trace(v, pos):
    n = v.shape[-1]
    return v.reshape(5, 64, n)[:, 48 * pos : 48 * pos + 16].reshape(FACE, n)


def b_trace(v, pos):
    n = v.shape[-1]
    tiles = v.reshape(10, 2, 2, 8, n)
    even = tiles[:, 0, pos].reshape(FACE, n)
    odd = tiles[:, 1, pos].reshape(FACE, n)
    lower = iota((FACE, n), 0) % 8 < 4
    if pos == 0:
        return jnp.where(lower, even, pltpu.roll(odd, 4, 0))
    return jnp.where(lower, pltpu.roll(even, FACE - 4, 0), odd)


def c_trace(ref, pos, layer):
    rows = pl.ds(3 * pos, FACE, stride=4)
    return jnp.concatenate([ref[2 * layer, rows, :], ref[2 * layer + 1, rows, :]], axis=1)


def get(ref, layer):
    return jnp.concatenate([ref[2 * layer], ref[2 * layer + 1]], axis=1)


def put(ref, layer, value):
    ref[2 * layer] = value[:, 0:128]
    ref[2 * layer + 1] = value[:, 128:256]


def placement(face):
    row = iota((ROWS, FACE), 0)
    col = iota((ROWS, FACE), 1)
    field, first, second = col // 16, col // 4 % 4, col % 4
    pos = 3 * (face % 2)
    if face // 2 == 0:
        node = pos * 16 + first * 4 + second
    elif face // 2 == 1:
        node = first * 16 + pos * 4 + second
    else:
        node = first * 16 + second * 4 + pos
    return (row == field * 64 + node).astype(BF16)


def layer_lanes(layer):
    return pl.ds(pl.multiple_of(layer * COLS, COLS), COLS)


def kernel(
    inter_hbm, cot_hbm, metric_hbm, volume_hbm, face_hbm, mask_hbm, out_hbm,
    inter, start, metric, volume, faces, mask_i,
    w, acc, lift, small, j3, face_out, face_in,
    rim_out, rim_in, s1, r1_first, r1_second, s2, r2_first, r2_second,
    local_sem, send_sem, recv_sem,
):
    c = lax.axis_index("comp")
    g = lax.axis_index("gx")
    y = lax.axis_index("gy")
    z, x = g // 4, g % 4
    last_y = lax.axis_size("gy") - 1
    other = 1 - c

    def place(comp, zz, xx):
        return {"comp": comp, "gx": zz * 4 + xx % 4, "gy": y}

    phase1 = [place(other, z, x + q) for q in range(4)]
    phase2 = [(zf, d, place(c, (z + zf) % 2, x + d)) for zf in range(2) for d in range(4) if zf or d]
    north = {"comp": c, "gx": g, "gy": jnp.minimum(y + 1, last_y)}
    south = {"comp": c, "gx": g, "gy": jnp.maximum(y - 1, 0)}

    barrier = pltpu.get_barrier_semaphore()
    for device in phase1 + [d for _, _, d in phase2]:
        pl.semaphore_signal(barrier, inc=1, device_id=device, device_id_type=MESH)

    @pl.when(y < last_y)
    def _():
        pl.semaphore_signal(barrier, inc=1, device_id=north, device_id_type=MESH)

    @pl.when(y > 0)
    def _():
        pl.semaphore_signal(barrier, inc=1, device_id=south, device_id_type=MESH)

    loads = [
        pltpu.make_async_copy(src, dst, local_sem.at[i])
        for i, (src, dst) in enumerate(
            [(cot_hbm.at[:, 128 * t : 128 * t + 128], start.at[t]) for t in range(8)]
            + [
                (mask_hbm, mask_i),
                (face_hbm, faces),
                (volume_hbm, volume),
                (metric_hbm, metric),
                (inter_hbm, inter),
            ]
        )
    ]
    for load in loads:
        load.start()

    surface = 3 * c
    r1, r2 = (r1_first, r1_second), (r2_first, r2_second)
    lane = iota((FACE, 128), 1)
    j3[...] = jnp.zeros_like(j3)

    for load in loads[0:9]:
        load.wait()
    mask = jnp.where(c == 0, 1.0, mask_i[...].astype(F32))

    def mask_start(layer, carry):
        put(start, layer, get(start, layer) * mask)
        return carry

    lax.fori_loop(0, LEV, mask_start, 0)

    def surface_trace(ref):
        return jnp.where(c == 0, c_trace(ref, 0, surface), c_trace(ref, 1, surface))

    def pack_block(block, dst):
        for q in range(4):
            dst[q, 0:40] = block[40 * (q % 2) : 40 * (q % 2) + 40, 128 * (q // 2) : 128 * (q // 2) + 128]

    def pack_rims(ref, dst):
        east = west = far = near = jnp.zeros((FACE, 128), F32)
        for layer in range(LEV):
            for half in range(2):
                v = ref[2 * layer + half]
                here = lane // 16 == layer
                if half == 1:
                    east = jnp.where(here, pltpu.roll(a_trace(v, 1), (16 * layer + 16) % 128, 1), east)
                else:
                    west = jnp.where(here, pltpu.roll(a_trace(v, 0), 16 * layer, 1), west)
                there = lane % 16 == layer + 4 * half
                far = jnp.where(there, pltpu.roll(b_trace(v, 1), (layer + 4 * half + 113) % 128, 1), far)
                near = jnp.where(there, pltpu.roll(b_trace(v, 0), layer + 4 * half, 1), near)
        dst[0], dst[1], dst[2], dst[3] = east, west, far, near

    count = [0]

    def remote(src, dst, device):
        k = count[0]
        count[0] += 1
        return pltpu.make_async_remote_copy(
            src_ref=src, dst_ref=dst, send_sem=send_sem.at[k], recv_sem=recv_sem.at[k],
            device_id=device, device_id_type=MESH,
        )

    pack_block(surface_trace(start), s1.at[0])
    pack_rims(start, rim_out.at[0])

    loads[9].wait()
    row = iota((FACE, SLOT), 0)
    col = iota((FACE, SLOT), 1)
    to_high = ((col == row) | (col == row + FACE)).astype(BF16)
    to_low = (col == row + 2 * FACE).astype(BF16)
    for face in range(6):
        scaled = STEP * faces[face]
        high = scaled.astype(BF16)
        low = (scaled - high.astype(F32)).astype(BF16)
        spread = jnp.dot(high, to_high, preferred_element_type=F32) + jnp.dot(
            low, to_low, preferred_element_type=F32
        )
        small[face] = spread.astype(BF16)
        lift[:, face * SLOT : face * SLOT + SLOT] = jnp.dot(
            placement(face), small[face], preferred_element_type=F32
        ).astype(BF16)
    face_out[...] = small[4 + c].astype(F32)

    loads[10].wait()
    loads[11].wait()
    loads[12].wait()

    off = inter[y]
    delta = jnp.where(c == 0, off, 8 - off) % 8
    shift = delta % 4
    z_from = (g + delta) % 8 // 4
    z_pick = jnp.where(z_from == z, 0, 1)

    pl.semaphore_wait(
        barrier, 11 + jnp.where(y < last_y, 1, 0) + jnp.where(y > 0, 1, 0)
    )

    swap_face = remote(face_out, face_in, phase1[0])
    piece = (40, 48)
    copies1, copies2, rims = [], [], []
    for m in range(2):
        part = pl.ds(0, piece[m])
        copies1.append([remote(s1.at[m, q, part], r1[m].at[q, part], phase1[q]) for q in range(4)])
        copies2.append([remote(s2.at[m, d, part], r2[m].at[zf, d, part], dev) for zf, d, dev in phase2])
        rims.append([
            remote(rim_out.at[m, 0], rim_in.at[m, 0], {"comp": c, "gx": (g + 1) % 8, "gy": y}),
            remote(rim_out.at[m, 1], rim_in.at[m, 1], {"comp": c, "gx": (g + 7) % 8, "gy": y}),
            remote(rim_out.at[m, 2], rim_in.at[m, 2], north),
            remote(rim_out.at[m, 3], rim_in.at[m, 3], south),
        ])

    def start_rims(m):
        rims[m][0].start()
        rims[m][1].start()

        @pl.when(y < last_y)
        def _():
            rims[m][2].start()

        @pl.when(y > 0)
        def _():
            rims[m][3].start()

    def wait_rims(m):
        rims[m][0].wait_recv()
        rims[m][1].wait_recv()

        @pl.when(y > 0)
        def _():
            rims[m][2].wait_recv()

        @pl.when(y == 0)
        def _():
            rim_in[m, 2] = jnp.zeros((FACE, 128), F32)

        @pl.when(y < last_y)
        def _():
            rims[m][3].wait_recv()

        @pl.when(y == last_y)
        def _():
            rim_in[m, 3] = jnp.zeros((FACE, 128), F32)

    def forward(m):
        for copy in copies1[m]:
            copy.wait_recv()
        for d in range(4):
            s2[m, d, 0 : piece[m]] = r1[m][(8 - d - shift) % 4, 0 : piece[m]]
        for copy in copies2[m]:
            copy.start()
        r2[m][0, 0, 0 : piece[m]] = s2[m, 0, 0 : piece[m]]

    def collect(m):
        for copy in copies2[m]:
            copy.wait_recv()
        q = [r2[m][z_pick, (8 - i - shift) % 4, 0 : piece[m]] for i in range(4)]
        left = jnp.concatenate([q[0][0:40], q[1][0:40]], axis=0)
        right = jnp.concatenate([q[2][0:40], q[3][0:40]], axis=0)
        wet = None if m == 0 else jnp.concatenate([q[0][40:41], q[2][40:41]], axis=1)
        return jnp.concatenate([left, right], axis=1), wet

    start_rims(0)
    for copy in copies1[0]:
        copy.start()
    swap_face.start()

    wide = iota((FACE, COLS), 1)

    def local(src, layer):
        lanes = layer_lanes(layer)
        v = get(src, layer)
        j3[0:SLOT] = split3(
            jnp.where(wide < 16, 0.0, pltpu.roll(a_trace(v, 1), 16, 1)) - a_trace(v, 0)
        )
        j3[SLOT : 2 * SLOT] = split3(
            jnp.where(wide >= 240, 0.0, pltpu.roll(a_trace(v, 0), 240, 1)) - a_trace(v, 1)
        )
        low, high = b_trace(v, 0), b_trace(v, 1)
        j3[2 * SLOT : 3 * SLOT] = split3(jnp.where(wide % 16 == 0, 0.0, pltpu.roll(high, 1, 1)) - low)
        j3[3 * SLOT : 4 * SLOT] = split3(jnp.where(wide % 16 == 15, 0.0, pltpu.roll(low, 255, 1)) - high)
        below = c_trace(src, 1, jnp.maximum(layer - 1, 0))
        above = c_trace(src, 0, jnp.minimum(layer + 1, LEV - 1))
        j3[4 * SLOT : 5 * SLOT] = split3(jnp.where(layer > 0, below, 0.0) - c_trace(src, 0, layer))
        j3[5 * SLOT :] = split3(jnp.where(layer < LEV - 1, above, 0.0) - c_trace(src, 1, layer))
        lifted = jnp.dot(lift[...], j3[...], preferred_element_type=F32)
        term = jnp.dot(volume[...], v.astype(BF16), preferred_element_type=F32)
        weight = STEP * metric[:, lanes]
        term = (term.reshape(5, 64, COLS) * weight[None]).reshape(ROWS, COLS)
        return (term + lifted) * mask

    def rim_part(m, layer):
        packed = [rim_in[m, k] for k in range(4)]
        west = jnp.where(lane < 16, pltpu.roll(packed[0], (128 - 16 * layer) % 128, 1), 0.0)
        east = jnp.where(lane >= 112, pltpu.roll(packed[1], 112 - 16 * layer, 1), 0.0)
        none = jnp.zeros((FACE, 128), F32)
        near, far = [], []
        for half in range(2):
            step = layer + 4 * half
            near.append(jnp.where(lane % 16 == 0, pltpu.roll(packed[2], (128 - step) % 128, 1), 0.0))
            far.append(jnp.where(lane % 16 == 15, pltpu.roll(packed[3], (143 - step) % 128, 1), 0.0))
        j3[0:SLOT] = split3(jnp.concatenate([west, none], axis=1))
        j3[SLOT : 2 * SLOT] = split3(jnp.concatenate([none, east], axis=1))
        j3[2 * SLOT : 3 * SLOT] = split3(jnp.concatenate(near, axis=1))
        j3[3 * SLOT : 4 * SLOT] = split3(jnp.concatenate(far, axis=1))
        return jnp.dot(
            lift[:, 0 : 4 * SLOT], j3[0 : 4 * SLOT], preferred_element_type=F32
        ) * mask

    def interface_part(block):
        op = lift[:, pl.ds(pl.multiple_of((4 + c) * SLOT, SLOT), SLOT)]
        return jnp.dot(op, split3(block), preferred_element_type=F32) * mask

    def first(layer, carry):
        put(w, layer, get(start, layer) + local(start, layer))
        return carry

    lax.fori_loop(0, LEV, first, 0)
    forward(0)
    wait_rims(0)

    def first_rims(layer, carry):
        put(w, layer, get(w, layer) + rim_part(0, layer))
        return carry

    lax.fori_loop(0, LEV, first_rims, 0)

    held = surface_trace(w)
    pack_block(held, s1.at[1])
    for q in range(4):
        s1[1, q, 40:48] = jnp.broadcast_to(mask[:, 128 * (q // 2) : 128 * (q // 2) + 128], (8, 128))
    for copy in copies1[1]:
        copy.start()
    swap_face.wait_recv()
    own = surface_trace(start)
    reply = jnp.dot(face_in[...].astype(BF16), split3(own), preferred_element_type=F32)
    forward(1)

    block, _ = collect(0)
    put(w, surface, get(w, surface) + interface_part(block))

    pack_rims(w, rim_out.at[1])
    start_rims(1)

    def second(layer, carry):
        put(acc, layer, get(start, layer) + get(w, layer) + local(w, layer))
        return carry

    lax.fori_loop(0, LEV, second, 0)
    wait_rims(1)

    def second_rims(layer, carry):
        put(acc, layer, 0.5 * (get(acc, layer) + rim_part(1, layer)))
        return carry

    lax.fori_loop(0, LEV, second_rims, 0)
    block, wet = collect(1)
    put(acc, surface, get(acc, surface) + 0.5 * interface_part(block + wet * reply))

    stores = [
        pltpu.make_async_copy(acc.at[t], out_hbm.at[:, 128 * t : 128 * t + 128], local_sem.at[13 + t])
        for t in range(8)
    ]
    for store in stores:
        store.start()
    for copies in [[swap_face]] + copies1 + copies2:
        for copy in copies:
            copy.wait_send()
    for m in range(2):
        rims[m][0].wait_send()
        rims[m][1].wait_send()

        @pl.when(y < last_y)
        def _():
            rims[m][2].wait_send()

        @pl.when(y > 0)
        def _():
            rims[m][3].wait_send()

    for store in stores:
        store.wait()


def body(cotangent, metric, volume_ops, face_ops, land_mask, intersection):
    copies = 31
    out = pl.pallas_call(
        kernel,
        out_shape=jax.ShapeDtypeStruct((ROWS, LEV * COLS), F32),
        in_specs=[pl.BlockSpec(memory_space=pl.ANY)] * 6,
        out_specs=pl.BlockSpec(memory_space=pl.ANY),
        scratch_shapes=[
            pltpu.SMEM((16,), jnp.int32),
            pltpu.VMEM((2 * LEV, ROWS, 128), F32),
            pltpu.VMEM((64, LEV * COLS), F32),
            pltpu.VMEM((ROWS, ROWS), BF16),
            pltpu.VMEM((6, FACE, FACE), F32),
            pltpu.VMEM((1, COLS), jnp.int32),
            pltpu.VMEM((2 * LEV, ROWS, 128), F32),
            pltpu.VMEM((2 * LEV, ROWS, 128), F32),
            pltpu.VMEM((ROWS, 6 * SLOT), BF16),
            pltpu.VMEM((6, FACE, SLOT), BF16),
            pltpu.VMEM((6 * SLOT, COLS), BF16),
            pltpu.VMEM((FACE, SLOT), F32),
            pltpu.VMEM((FACE, SLOT), F32),
            pltpu.VMEM((2, 4, FACE, 128), F32),
            pltpu.VMEM((2, 4, FACE, 128), F32),
            pltpu.VMEM((2, 4, 48, 128), F32),
            pltpu.VMEM((4, 40, 128), F32),
            pltpu.VMEM((4, 48, 128), F32),
            pltpu.VMEM((2, 4, 48, 128), F32),
            pltpu.VMEM((2, 4, 40, 128), F32),
            pltpu.VMEM((2, 4, 48, 128), F32),
            pltpu.SemaphoreType.DMA((21,)),
            pltpu.SemaphoreType.DMA((copies,)),
            pltpu.SemaphoreType.DMA((copies,)),
        ],
        compiler_params=pltpu.CompilerParams(
            collective_id=0, has_side_effects=True, vmem_limit_bytes=48 * 1024 * 1024
        ),
    )(
        intersection,
        cotangent[0, 0, 0],
        metric[0, 0, 0],
        volume_ops[0],
        face_ops[0],
        land_mask[0],
    )
    return out[None, None, None]


def solution(mesh):
    in_specs = (
        P("comp", "gx", "gy", None, None),
        P("comp", "gx", "gy", None, None),
        P("comp", None, None),
        P("comp", None, None, None),
        P("gx", "gy", None),
        P(),
    )
    out_specs = P("comp", "gx", "gy", None, None)
    return jax.shard_map(body, mesh=mesh, in_specs=in_specs, out_specs=out_specs, check_vma=False)
```

```python
import functools

import jax
import jax.numpy as jnp
from jax import lax
from jax.experimental import pallas as pl
from jax.experimental.pallas import tpu as pltpu
from jax.sharding import PartitionSpec as P

MESH = pl.DeviceIdType.MESH
F32 = jnp.float32
BF16 = jnp.bfloat16
ROWS = 320
COLS = 256
LEV = 4
FACE = 80
SLOT = 256
STEP = 0.4


def iota(shape, axis):
    return lax.broadcasted_iota(jnp.int32, shape, axis)


def split3(x):
    high = x.astype(BF16)
    low = (x - high.astype(F32)).astype(BF16)
    return jnp.concatenate([high, low, high, jnp.zeros((16, x.shape[1]), BF16)], axis=0)


def a_trace(v, pos):
    n = v.shape[-1]
    return v.reshape(5, 64, n)[:, 48 * pos : 48 * pos + 16].reshape(FACE, n)


def b_trace(v, pos):
    n = v.shape[-1]
    tiles = v.reshape(10, 2, 2, 8, n)
    even = tiles[:, 0, pos].reshape(FACE, n)
    odd = tiles[:, 1, pos].reshape(FACE, n)
    lower = iota((FACE, n), 0) % 8 < 4
    if pos == 0:
        return jnp.where(lower, even, pltpu.roll(odd, 4, 0))
    return jnp.where(lower, pltpu.roll(even, FACE - 4, 0), odd)


def c_trace(ref, pos, layer):
    rows = pl.ds(3 * pos, FACE, stride=4)
    return jnp.concatenate([ref[2 * layer, rows, :], ref[2 * layer + 1, rows, :]], axis=1)


def get(ref, layer):
    return jnp.concatenate([ref[2 * layer], ref[2 * layer + 1]], axis=1)


def put(ref, layer, value):
    ref[2 * layer] = value[:, 0:128]
    ref[2 * layer + 1] = value[:, 128:256]


def placement(face):
    row = iota((ROWS, FACE), 0)
    col = iota((ROWS, FACE), 1)
    field, first, second = col // 16, col // 4 % 4, col % 4
    pos = 3 * (face % 2)
    if face // 2 == 0:
        node = pos * 16 + first * 4 + second
    elif face // 2 == 1:
        node = first * 16 + pos * 4 + second
    else:
        node = first * 16 + second * 4 + pos
    return (row == field * 64 + node).astype(BF16)


def fold_x(v):
    lane = iota((8, 128), 1)
    out = [jnp.zeros((8, 128), F32)] * 2
    for r in range(10):
        j = r % 8
        out[r // 8] = jnp.where(lane // 16 == j, pltpu.roll(v[8 * r : 8 * r + 8], 16 * j, 1), out[r // 8])
    return jnp.concatenate(out, axis=0)


def unfold_x(v):
    tiles = []
    for r in range(10):
        part = v[r // 8 * 8 : r // 8 * 8 + 8]
        tiles.append(pltpu.roll(part, (128 - 16 * (r % 8)) % 128, 1))
    return jnp.concatenate(tiles, axis=0)


def fold_y(v):
    lane = iota((8, 128), 1)
    out = [jnp.zeros((8, 128), F32)] * 2
    for r in range(10):
        j = r % 8
        out[r // 8] = jnp.where(lane % 16 // 2 == j, pltpu.roll(v[8 * r : 8 * r + 8], 2 * j, 1), out[r // 8])
    return jnp.concatenate(out, axis=0)


def unfold_y(v):
    tiles = []
    for r in range(10):
        part = v[r // 8 * 8 : r // 8 * 8 + 8]
        tiles.append(pltpu.roll(part, (128 - 2 * (r % 8)) % 128, 1))
    return jnp.concatenate(tiles, axis=0)


def fold_half(v, by):
    lane = iota((40, 128), 1)
    return jnp.where(lane % (2 * by) < by, v[0:40], pltpu.roll(v[40:80], by, 1))


def unfold_half(v, by):
    return jnp.concatenate([v, pltpu.roll(v, 128 - by, 1)], axis=0)


def layer_lanes(layer):
    return pl.ds(pl.multiple_of(layer * COLS, COLS), COLS)


def kernel(
    inter_hbm, cot_hbm, metric_hbm, volume_hbm, face_hbm, mask_hbm, acc,
    inter, start, metric, volume, faces, mask_i,
    w, lift, small, j3, face_out, face_in,
    rim_out, rim_in, s1, r1, s2, r2, ua_out, ua_in, ub_out, ub_in,
    patch_rows, patch_out, patch_in, side_out, side_in, edge_out, edge_in, rim_edge, rim_full,
    local_sem, send_sem, recv_sem, side_sem,
):
    c = lax.axis_index("comp")
    g = lax.axis_index("gx")
    y = lax.axis_index("gy")
    z, x = g // 4, g % 4
    last_y = lax.axis_size("gy") - 1
    other = 1 - c

    def place(comp, zz, xx):
        return {"comp": comp, "gx": zz * 4 + xx % 4, "gy": y}

    mates = [(zf, d, place(other, (z + zf) % 2, x + d)) for zf in range(2) for d in range(4)]
    phase1 = [place(other, z, x + q) for q in range(4)]
    phase2 = [(zf, d, place(c, (z + zf) % 2, x + d)) for zf in range(2) for d in range(4) if zf or d]
    north = {"comp": c, "gx": g, "gy": jnp.minimum(y + 1, last_y)}
    south = {"comp": c, "gx": g, "gy": jnp.maximum(y - 1, 0)}

    barrier = pltpu.get_barrier_semaphore()
    for device in [d for _, _, d in mates + phase2]:
        pl.semaphore_signal(barrier, inc=1, device_id=device, device_id_type=MESH)

    @pl.when(y < last_y)
    def _():
        pl.semaphore_signal(barrier, inc=1, device_id=north, device_id_type=MESH)

    @pl.when(y > 0)
    def _():
        pl.semaphore_signal(barrier, inc=1, device_id=south, device_id_type=MESH)

    loads = [
        pltpu.make_async_copy(src, dst, local_sem.at[i])
        for i, (src, dst) in enumerate(
            [(cot_hbm.at[:, 128 * t : 128 * t + 128], start.at[t]) for t in range(8)]
            + [
                (mask_hbm, mask_i),
                (face_hbm, faces),
                (volume_hbm, volume),
                (metric_hbm, metric),
                (inter_hbm, inter),
            ]
        )
    ]
    for load in loads:
        load.start()

    surface = 3 * c
    lane = iota((FACE, 128), 1)
    j3[...] = jnp.zeros_like(j3)

    for load in loads[0:9]:
        load.wait()
    mask = jnp.where(c == 0, 1.0, mask_i[...].astype(F32))

    def mask_start(layer, carry):
        put(start, layer, get(start, layer) * mask)
        return carry

    lax.fori_loop(0, LEV, mask_start, 0)

    def surface_trace(ref):
        return jnp.where(c == 0, c_trace(ref, 0, surface), c_trace(ref, 1, surface))

    def pack_block(block, dst):
        for q in range(4):
            dst[q, 0:40] = block[40 * (q % 2) : 40 * (q % 2) + 40, 128 * (q // 2) : 128 * (q // 2) + 128]

    def pack_rims(ref, dst):
        east = west = far = near = jnp.zeros((FACE, 128), F32)
        for layer in range(LEV):
            for half in range(2):
                v = ref[2 * layer + half]
                here = lane // 16 == layer
                if half == 1:
                    east = jnp.where(here, pltpu.roll(a_trace(v, 1), (16 * layer + 16) % 128, 1), east)
                else:
                    west = jnp.where(here, pltpu.roll(a_trace(v, 0), 16 * layer, 1), west)
                there = lane % 16 == layer + 4 * half
                far = jnp.where(there, pltpu.roll(b_trace(v, 1), (layer + 4 * half + 113) % 128, 1), far)
                near = jnp.where(there, pltpu.roll(b_trace(v, 0), layer + 4 * half, 1), near)
        dst[0, 0:40], dst[1, 0:40] = fold_half(east, 64), fold_half(west, 64)
        dst[2, 0:40], dst[3, 0:40] = fold_half(far, 8), fold_half(near, 8)

    count = [0]

    def remote(src, dst, device):
        k = count[0]
        count[0] += 1
        return pltpu.make_async_remote_copy(
            src_ref=src, dst_ref=dst, send_sem=send_sem.at[k], recv_sem=recv_sem.at[k],
            device_id=device, device_id_type=MESH,
        )

    own = surface_trace(start)
    pack_block(own, s1)
    pack_rims(start, rim_out.at[0])
    rim_out[0, 0, 40:48] = jnp.broadcast_to(pltpu.roll(mask[:, 128:256], 16, 1), (8, 128))
    rim_out[0, 1, 40:48] = jnp.broadcast_to(mask[:, 0:128], (8, 128))
    side_out[0] = fold_x(pltpu.roll(own[:, 128:256], 16, 1))
    side_out[1] = fold_x(own[:, 0:128])

    loads[9].wait()
    row = iota((FACE, SLOT), 0)
    col = iota((FACE, SLOT), 1)
    to_high = ((col == row) | (col == row + FACE)).astype(BF16)
    to_low = (col == row + 2 * FACE).astype(BF16)
    for face in range(6):
        scaled = STEP * faces[face]
        high = scaled.astype(BF16)
        low = (scaled - high.astype(F32)).astype(BF16)
        spread = jnp.dot(high, to_high, preferred_element_type=F32) + jnp.dot(
            low, to_low, preferred_element_type=F32
        )
        small[face] = spread.astype(BF16)
        lift[:, face * SLOT : face * SLOT + SLOT] = jnp.dot(
            placement(face), small[face], preferred_element_type=F32
        ).astype(BF16)
    face_out[...] = small[4 + c].astype(F32)

    loads[10].wait()
    loads[11].wait()
    loads[12].wait()

    off = inter[y]
    delta = jnp.where(c == 0, off, 8 - off) % 8
    shift = delta % 4
    z_from = (g + delta) % 8 // 4
    z_pick = jnp.where(z_from == z, 0, 1)

    swap_face = remote(face_out, face_in, mates[0][2])
    copies1 = [remote(s1.at[q], r1.at[q], phase1[q]) for q in range(4)]
    copies2 = [remote(s2.at[d], r2.at[zf, d], dev) for zf, d, dev in phase2]
    uas = [remote(ua_out.at[d], ua_in.at[zf, d], dev) for zf, d, dev in mates]
    ubs = [remote(ub_out.at[d], ub_in.at[d], place(c, z, x + d)) for d in range(1, 4)]
    patches = [remote(patch_out, patch_in.at[zf, d], dev) for zf, d, dev in mates]
    around = [
        {"comp": c, "gx": (g + 1) % 8, "gy": y},
        {"comp": c, "gx": (g + 7) % 8, "gy": y},
        north,
        south,
    ]
    rims = [
        [remote(rim_out.at[m, k, part], rim_in.at[m, k, part], around[k])
         for k, part in enumerate([pl.ds(0, 48)] * 2 + [pl.ds(0, 40)] * 2)]
        for m in range(2)
    ]
    edges = [remote(edge_out.at[k], edge_in.at[k], around[k]) for k in range(4)]
    sides = []
    base = count[0]
    for k in range(2):
        for zz in range(2):
            n = 2 * k + zz
            sides.append(pltpu.make_async_remote_copy(
                src_ref=side_out.at[k], dst_ref=side_in.at[g], send_sem=send_sem.at[base + n],
                recv_sem=side_sem.at[g], device_id=place(other, zz, 3 * k), device_id_type=MESH,
            ))
    sides_in = [
        pltpu.make_async_remote_copy(
            src_ref=side_out.at[0], dst_ref=side_in.at[i], send_sem=send_sem.at[base],
            recv_sem=side_sem.at[i], device_id=mates[0][2], device_id_type=MESH,
        )
        for i in range(8)
    ]
    has = [x < 3, x > 0, y < last_y, y > 0]
    gets = [x > 0, x < 3, y > 0, y < last_y]

    def start_rims(m):
        rims[m][0].start()
        rims[m][1].start()
        for k in (2, 3):
            pl.when(has[k])(rims[m][k].start)

    def wait_rims(m):
        rims[m][0].wait_recv()
        rims[m][1].wait_recv()
        for k in (2, 3):
            pl.when(gets[k])(rims[m][k].wait_recv)

            @pl.when(jnp.logical_not(gets[k]))
            def _():
                rim_in[m, k] = jnp.zeros((48, 128), F32)

    def forward():
        for copy in copies1:
            copy.wait_recv()
        for d in range(4):
            s2[d] = r1[(8 - d - shift) % 4]
        for copy in copies2:
            copy.start()
        r2[0, 0] = s2[0]

    def joined(q):
        left = jnp.concatenate([q[0][0:40], q[1][0:40]], axis=0)
        right = jnp.concatenate([q[2][0:40], q[3][0:40]], axis=0)
        return jnp.concatenate([left, right], axis=1)

    def collect():
        for copy in copies2:
            copy.wait_recv()
        return joined([r2[z_pick, (8 - i - shift) % 4] for i in range(4)])

    def forward_base():
        for copy in uas:
            copy.wait_recv()
        for d in range(4):
            z_of = (z * 4 + (x + d) % 4 + delta) % 8 // 4
            ub_out[d] = ua_in[jnp.where(z_of == z, 0, 1), (8 - d - shift) % 4]
        for copy in ubs:
            copy.start()
        ub_in[0] = ub_out[0]

    wide = iota((FACE, COLS), 1)

    def local(src, layer):
        lanes = layer_lanes(layer)
        v = get(src, layer)
        j3[0:SLOT] = split3(
            jnp.where(wide < 16, 0.0, pltpu.roll(a_trace(v, 1), 16, 1)) - a_trace(v, 0)
        )
        j3[SLOT : 2 * SLOT] = split3(
            jnp.where(wide >= 240, 0.0, pltpu.roll(a_trace(v, 0), 240, 1)) - a_trace(v, 1)
        )
        low, high = b_trace(v, 0), b_trace(v, 1)
        j3[2 * SLOT : 3 * SLOT] = split3(jnp.where(wide % 16 == 0, 0.0, pltpu.roll(high, 1, 1)) - low)
        j3[3 * SLOT : 4 * SLOT] = split3(jnp.where(wide % 16 == 15, 0.0, pltpu.roll(low, 255, 1)) - high)
        below = c_trace(src, 1, jnp.maximum(layer - 1, 0))
        above = c_trace(src, 0, jnp.minimum(layer + 1, LEV - 1))
        j3[4 * SLOT : 5 * SLOT] = split3(jnp.where(layer > 0, below, 0.0) - c_trace(src, 0, layer))
        j3[5 * SLOT :] = split3(jnp.where(layer < LEV - 1, above, 0.0) - c_trace(src, 1, layer))
        lifted = jnp.dot(lift[...], j3[...], preferred_element_type=F32)
        term = jnp.dot(volume[...], v.astype(BF16), preferred_element_type=F32)
        weight = STEP * metric[:, lanes]
        term = (term.reshape(5, 64, COLS) * weight[None]).reshape(ROWS, COLS)
        return (term + lifted) * mask

    def rim_lift(west, east, near, far):
        none = jnp.zeros((FACE, 128), F32)
        j3[0:SLOT] = split3(jnp.concatenate([jnp.where(lane < 16, west, 0.0), none], axis=1))
        j3[SLOT : 2 * SLOT] = split3(jnp.concatenate([none, jnp.where(lane >= 112, east, 0.0)], axis=1))
        near = [jnp.where(lane % 16 == 0, v, 0.0) for v in near]
        far = [jnp.where(lane % 16 == 15, v, 0.0) for v in far]
        j3[2 * SLOT : 3 * SLOT] = split3(jnp.concatenate(near, axis=1))
        j3[3 * SLOT : 4 * SLOT] = split3(jnp.concatenate(far, axis=1))
        return jnp.dot(
            lift[:, 0 : 4 * SLOT], j3[0 : 4 * SLOT], preferred_element_type=F32
        ) * mask

    def unfold_rims(m):
        for k in range(4):
            rim_full[k] = unfold_half(rim_in[m, k, 0:40], 64 if k < 2 else 8)

    def rim_part(layer):
        return rim_lift(
            pltpu.roll(rim_full[0], (128 - 16 * layer) % 128, 1),
            pltpu.roll(rim_full[1], 112 - 16 * layer, 1),
            [pltpu.roll(rim_full[2], (128 - layer - 4 * h) % 128, 1) for h in range(2)],
            [pltpu.roll(rim_full[3], (143 - layer - 4 * h) % 128, 1) for h in range(2)],
        )

    def interface_part(block):
        op = lift[:, pl.ds(pl.multiple_of((4 + c) * SLOT, SLOT), SLOT)]
        return jnp.dot(op, split3(block), preferred_element_type=F32) * mask

    def first(layer):
        put(w, layer, get(start, layer) + local(start, layer))

    first(surface)
    held = surface_trace(w)
    pack_block(held, ua_out)
    for q in range(4):
        ua_out[q, 40:48] = jnp.broadcast_to(mask[:, 128 * (q // 2) : 128 * (q // 2) + 128], (8, 128))

    pl.semaphore_wait(
        barrier, 15 + jnp.where(y < last_y, 1, 0) + jnp.where(y > 0, 1, 0)
    )

    start_rims(0)
    for copy in copies1 + uas + sides + [swap_face]:
        copy.start()

    def others(step):
        def run(i, carry):
            step(i + 1 - c)
            return carry

        lax.fori_loop(0, LEV - 1, run, 0)

    others(first)
    forward()

    wait_rims(0)
    unfold_rims(0)
    here = (128 - 3 * c) % 128
    level = [
        pltpu.roll(rim_full[0], (128 - 48 * c) % 128, 1),
        pltpu.roll(rim_full[1], (128 - 48 * c) % 128, 1),
    ] + [
        jnp.where(lane % 16 == 0, pltpu.roll(rim_full[k], here, 1), pltpu.roll(rim_full[k], (125 - 3 * c) % 128, 1))
        for k in (2, 3)
    ]
    for k in range(4):
        patch_rows[FACE * k : FACE * k + FACE] = jnp.dot(
            small[k], split3(level[k]), preferred_element_type=F32
        )
    nodes = jnp.where(
        c == 0, patch_rows[pl.ds(0, FACE, stride=4), :], patch_rows[pl.ds(3, FACE, stride=4), :]
    )
    lane8 = iota((8, 128), 1)
    folded = [jnp.zeros((8, 128), F32)] * 2
    for r in range(5):
        tile = nodes[8 * r : 8 * r + 8]
        folded[0] = jnp.where(lane8 // 16 == r, pltpu.roll(tile, 16 * r, 1), folded[0])
        tile = nodes[40 + 8 * r : 48 + 8 * r]
        folded[1] = jnp.where(lane8 % 16 // 2 == r, pltpu.roll(tile, 2 * r, 1), folded[1])
    patch_out[...] = jnp.concatenate(folded, axis=0)
    for copy in patches:
        copy.start()

    def first_rims(layer, carry):
        put(w, layer, get(w, layer) + rim_part(layer))
        return carry

    lax.fori_loop(0, LEV, first_rims, 0)
    pack_rims(w, rim_out.at[1])
    start_rims(1)

    swap_face.wait_recv()
    reply = jnp.dot(face_in[...].astype(BF16), split3(surface_trace(start)), preferred_element_type=F32)

    def second(layer):
        acc[:, layer_lanes(layer)] = get(start, layer) + get(w, layer) + local(w, layer)

    others(second)
    forward_base()

    put(w, surface, get(w, surface) + interface_part(collect()))

    v0, v1 = w[2 * surface], w[2 * surface + 1]
    first_two = lane % 16 == 0
    edge_out[0] = fold_x(pltpu.roll(a_trace(v1, 1), 16, 1))
    edge_out[1] = fold_x(a_trace(v0, 0))
    edge_out[2] = fold_y(
        jnp.where(first_two, pltpu.roll(b_trace(v0, 1), 113, 1), pltpu.roll(b_trace(v1, 1), 114, 1))
    )
    edge_out[3] = fold_y(jnp.where(first_two, b_trace(v0, 0), pltpu.roll(b_trace(v1, 0), 1, 1)))
    for k in range(4):
        pl.when(has[k])(edges[k].start)

    second(surface)
    wait_rims(1)
    unfold_rims(1)

    def second_rims(layer):
        lanes = layer_lanes(layer)
        acc[:, lanes] = 0.5 * (acc[:, lanes] + rim_part(layer))

    others(second_rims)

    def finish_edge(k):
        for copy in sides_in:
            copy.wait_recv()
        partner = (g + (7 if k == 0 else 1) + delta) % 8
        row = iota((FACE, FACE), 0)
        col = iota((FACE, FACE), 1)
        pick = (
            (row // 16 == col // 16) & (row % 4 == 3 * c) & (col % 4 == row // 4 % 4)
            & (col // 4 % 4 == (3 if k == 0 else 0))
        ).astype(BF16)
        op = jnp.dot(pick, small[4 + c], preferred_element_type=F32).astype(BF16)
        term = jnp.dot(op, split3(unfold_x(side_in[partner])), preferred_element_type=F32)
        held = pltpu.roll(rim_full[k], (128 - 48 * c) % 128, 1)
        rim_edge[k] = held + term * rim_in[0, k, 40:41]

    def take_edge(k):
        edges[k].wait_recv()
        rim_edge[k] = unfold_x(edge_in[k]) if k < 2 else unfold_y(edge_in[k])

    for k in range(4):
        pl.when(gets[k])(functools.partial(take_edge, k))

        @pl.when(jnp.logical_not(gets[k]))
        def _():
            if k < 2:
                finish_edge(k)
            else:
                rim_edge[k] = jnp.zeros((FACE, 128), F32)

    part = rim_lift(
        rim_edge[0],
        pltpu.roll(rim_edge[1], 112, 1),
        [rim_edge[2], pltpu.roll(rim_edge[2], 127, 1)],
        [pltpu.roll(rim_edge[3], 15, 1), pltpu.roll(rim_edge[3], 14, 1)],
    )
    lanes = layer_lanes(surface)
    acc[:, lanes] = 0.5 * (acc[:, lanes] + part)

    for copy in ubs + patches:
        copy.wait_recv()
    q = [ub_in[(8 - i - shift) % 4] for i in range(4)]
    wet = jnp.concatenate([q[0][40:41], q[2][40:41]], axis=1)
    patch = patch_in[z_pick, (4 - shift) % 4]
    tiles = [pltpu.roll(patch[0:8], (128 - 16 * r) % 128, 1) for r in range(5)]
    tiles += [pltpu.roll(patch[8:16], (128 - 2 * r) % 128, 1) for r in range(5)]
    packed = jnp.concatenate(tiles, axis=0)
    high = packed.astype(BF16)
    low = (packed - high.astype(F32)).astype(BF16)
    row = iota((2 * FACE, FACE), 0)
    col = iota((2 * FACE, FACE), 1)
    node, face, index = row % FACE, col // 20, col % 20
    target = index // 4 * 16 + jnp.where(face < 2, index % 4 + 12 * face, index % 4 * 4 + 3 * (face - 2))
    to_node = ((node == target) & (row // FACE == face // 2)).astype(BF16)
    spread = jnp.dot(to_node, high, preferred_element_type=F32) + jnp.dot(
        to_node, low, preferred_element_type=F32
    )
    on_x, on_y = spread[0:FACE], spread[FACE:]
    node = iota((FACE, 128), 0)
    node_a, node_b = node // 4 % 4, node % 4
    halves = []
    for h in range(2):
        side = (
            jnp.where((lane < 16) & (node_a == 0), on_x, 0.0)
            if h == 0
            else jnp.where((lane >= 112) & (node_a == 3), pltpu.roll(on_x, 112, 1), 0.0)
        )
        near = jnp.where((lane % 16 == 0) & (node_b == 0), pltpu.roll(on_y, (128 - h) % 128, 1), 0.0)
        far = jnp.where((lane % 16 == 15) & (node_b == 3), pltpu.roll(on_y, 15 - h, 1), 0.0)
        halves.append(side + near + far)
    block = joined(q) + wet * (jnp.concatenate(halves, axis=1) + reply)
    acc[:, lanes] = acc[:, lanes] + 0.5 * interface_part(block)

    for copy in [swap_face] + copies1 + copies2 + uas + ubs + patches + sides:
        copy.wait_send()
    for m in range(2):
        rims[m][0].wait_send()
        rims[m][1].wait_send()
        for k in (2, 3):
            pl.when(has[k])(rims[m][k].wait_send)
    for k in range(4):
        pl.when(has[k])(edges[k].wait_send)


def body(cotangent, metric, volume_ops, face_ops, land_mask, intersection):
    copies = 47
    out = pl.pallas_call(
        kernel,
        out_shape=jax.ShapeDtypeStruct((ROWS, LEV * COLS), F32),
        in_specs=[pl.BlockSpec(memory_space=pltpu.HBM)] * 6,
        out_specs=pl.BlockSpec(memory_space=pltpu.VMEM),
        scratch_shapes=[
            pltpu.SMEM((16,), jnp.int32),
            pltpu.VMEM((2 * LEV, ROWS, 128), F32),
            pltpu.VMEM((64, LEV * COLS), F32),
            pltpu.VMEM((ROWS, ROWS), BF16),
            pltpu.VMEM((6, FACE, FACE), F32),
            pltpu.VMEM((1, COLS), jnp.int32),
            pltpu.VMEM((2 * LEV, ROWS, 128), F32),
            pltpu.VMEM((ROWS, 6 * SLOT), BF16),
            pltpu.VMEM((6, FACE, SLOT), BF16),
            pltpu.VMEM((6 * SLOT, COLS), BF16),
            pltpu.VMEM((FACE, SLOT), F32),
            pltpu.VMEM((FACE, SLOT), F32),
            pltpu.VMEM((2, 4, 48, 128), F32),
            pltpu.VMEM((2, 4, 48, 128), F32),
            pltpu.VMEM((4, 40, 128), F32),
            pltpu.VMEM((4, 40, 128), F32),
            pltpu.VMEM((4, 40, 128), F32),
            pltpu.VMEM((2, 4, 40, 128), F32),
            pltpu.VMEM((4, 48, 128), F32),
            pltpu.VMEM((2, 4, 48, 128), F32),
            pltpu.VMEM((4, 48, 128), F32),
            pltpu.VMEM((4, 48, 128), F32),
            pltpu.VMEM((ROWS, 128), F32),
            pltpu.VMEM((16, 128), F32),
            pltpu.VMEM((2, 4, 16, 128), F32),
            pltpu.VMEM((2, 16, 128), F32),
            pltpu.VMEM((8, 16, 128), F32),
            pltpu.VMEM((4, 16, 128), F32),
            pltpu.VMEM((4, 16, 128), F32),
            pltpu.VMEM((4, FACE, 128), F32),
            pltpu.VMEM((4, FACE, 128), F32),
            pltpu.SemaphoreType.DMA((13,)),
            pltpu.SemaphoreType.DMA((copies,)),
            pltpu.SemaphoreType.DMA((copies,)),
            pltpu.SemaphoreType.DMA((8,)),
        ],
        compiler_params=pltpu.CompilerParams(
            collective_id=0, has_side_effects=True, vmem_limit_bytes=48 * 1024 * 1024
        ),
    )(
        *(
            pltpu.with_memory_space_constraint(a, pltpu.HBM)
            for a in (
                intersection,
                cotangent[0, 0, 0],
                metric[0, 0, 0],
                volume_ops[0],
                face_ops[0],
                land_mask[0],
            )
        )
    )
    return out[None, None, None]


def solution(mesh):
    in_specs = (
        P("comp", "gx", "gy", None, None),
        P("comp", "gx", "gy", None, None),
        P("comp", None, None),
        P("comp", None, None, None),
        P("gx", "gy", None),
        P(),
    )
    out_specs = P("comp", "gx", "gy", None, None)
    return jax.shard_map(body, mesh=mesh, in_specs=in_specs, out_specs=out_specs, check_vma=False)
```

```python
import functools

import jax
import jax.numpy as jnp
from jax import lax
from jax.experimental import pallas as pl
from jax.experimental.pallas import tpu as pltpu
from jax.sharding import PartitionSpec as P

MESH = pl.DeviceIdType.MESH
F32 = jnp.float32
BF16 = jnp.bfloat16
ROWS = 320
COLS = 256
LEV = 4
FACE = 80
SLOT = 256
STEP = 0.4


def iota(shape, axis):
    return lax.broadcasted_iota(jnp.int32, shape, axis)


def split3(x):
    high = x.astype(BF16)
    low = (x - high.astype(F32)).astype(BF16)
    return jnp.concatenate([high, low, high, jnp.zeros((16, x.shape[1]), BF16)], axis=0)


def a_trace(v, pos):
    n = v.shape[-1]
    return v.reshape(5, 64, n)[:, 48 * pos : 48 * pos + 16].reshape(FACE, n)


def b_trace(v, pos):
    n = v.shape[-1]
    tiles = v.reshape(10, 2, 2, 8, n)
    even = tiles[:, 0, pos].reshape(FACE, n)
    odd = tiles[:, 1, pos].reshape(FACE, n)
    lower = iota((FACE, n), 0) % 8 < 4
    if pos == 0:
        return jnp.where(lower, even, pltpu.roll(odd, 4, 0))
    return jnp.where(lower, pltpu.roll(even, FACE - 4, 0), odd)


def c_trace(ref, pos, layer):
    rows = pl.ds(3 * pos, FACE, stride=4)
    return jnp.concatenate([ref[2 * layer, rows, :], ref[2 * layer + 1, rows, :]], axis=1)


def get(ref, layer):
    return jnp.concatenate([ref[2 * layer], ref[2 * layer + 1]], axis=1)


def put(ref, layer, value):
    ref[2 * layer] = value[:, 0:128]
    ref[2 * layer + 1] = value[:, 128:256]


def placement(face):
    row = iota((ROWS, FACE), 0)
    col = iota((ROWS, FACE), 1)
    field, first, second = col // 16, col // 4 % 4, col % 4
    pos = 3 * (face % 2)
    if face // 2 == 0:
        node = pos * 16 + first * 4 + second
    elif face // 2 == 1:
        node = first * 16 + pos * 4 + second
    else:
        node = first * 16 + second * 4 + pos
    return (row == field * 64 + node).astype(BF16)


def fold_x(v):
    lane = iota((8, 128), 1)
    out = [jnp.zeros((8, 128), F32)] * 2
    for r in range(10):
        j = r % 8
        out[r // 8] = jnp.where(lane // 16 == j, pltpu.roll(v[8 * r : 8 * r + 8], 16 * j, 1), out[r // 8])
    return jnp.concatenate(out, axis=0)


def unfold_x(v):
    tiles = []
    for r in range(10):
        part = v[r // 8 * 8 : r // 8 * 8 + 8]
        tiles.append(pltpu.roll(part, (128 - 16 * (r % 8)) % 128, 1))
    return jnp.concatenate(tiles, axis=0)


def fold_y(v):
    lane = iota((8, 128), 1)
    out = [jnp.zeros((8, 128), F32)] * 2
    for r in range(10):
        j = r % 8
        out[r // 8] = jnp.where(lane % 16 // 2 == j, pltpu.roll(v[8 * r : 8 * r + 8], 2 * j, 1), out[r // 8])
    return jnp.concatenate(out, axis=0)


def unfold_y(v):
    tiles = []
    for r in range(10):
        part = v[r // 8 * 8 : r // 8 * 8 + 8]
        tiles.append(pltpu.roll(part, (128 - 2 * (r % 8)) % 128, 1))
    return jnp.concatenate(tiles, axis=0)


def fold_half(v, by):
    lane = iota((40, 128), 1)
    return jnp.where(lane % (2 * by) < by, v[0:40], pltpu.roll(v[40:80], by, 1))


def unfold_half(v, by):
    return jnp.concatenate([v, pltpu.roll(v, 128 - by, 1)], axis=0)


def layer_lanes(layer):
    return pl.ds(pl.multiple_of(layer * COLS, COLS), COLS)


def kernel(
    inter_hbm, cot_hbm, metric_hbm, volume_hbm, face_hbm, mask_hbm, acc,
    inter, start, metric, volume, faces, mask_i,
    w, lift, small, j3, face_out, face_in,
    rim_out, rim_in, s1, r1, s2, r2, ua_out, ua_in, ub_out, ub_in,
    patch_rows, patch_out, patch_in, side_out, side_in, edge_out, edge_in, rim_edge, terms,
    local_sem, send_sem, recv_sem, side_sem,
):
    c = lax.axis_index("comp")
    g = lax.axis_index("gx")
    y = lax.axis_index("gy")
    z, x = g // 4, g % 4
    last_y = lax.axis_size("gy") - 1
    other = 1 - c

    def place(comp, zz, xx):
        return {"comp": comp, "gx": zz * 4 + xx % 4, "gy": y}

    mates = [(zf, d, place(other, (z + zf) % 2, x + d)) for zf in range(2) for d in range(4)]
    phase1 = [place(other, z, x + q) for q in range(4)]
    phase2 = [(zf, d, place(c, (z + zf) % 2, x + d)) for zf in range(2) for d in range(4) if zf or d]
    north = {"comp": c, "gx": g, "gy": jnp.minimum(y + 1, last_y)}
    south = {"comp": c, "gx": g, "gy": jnp.maximum(y - 1, 0)}

    barrier = pltpu.get_barrier_semaphore()
    for device in [d for _, _, d in mates + phase2]:
        pl.semaphore_signal(barrier, inc=1, device_id=device, device_id_type=MESH)

    @pl.when(y < last_y)
    def _():
        pl.semaphore_signal(barrier, inc=1, device_id=north, device_id_type=MESH)

    @pl.when(y > 0)
    def _():
        pl.semaphore_signal(barrier, inc=1, device_id=south, device_id_type=MESH)

    loads = [
        pltpu.make_async_copy(src, dst, local_sem.at[i])
        for i, (src, dst) in enumerate(
            [(cot_hbm.at[:, 128 * t : 128 * t + 128], start.at[t]) for t in range(8)]
            + [
                (mask_hbm, mask_i),
                (face_hbm, faces),
                (volume_hbm, volume),
                (metric_hbm, metric),
                (inter_hbm, inter),
            ]
        )
    ]
    for load in loads:
        load.start()

    surface = 3 * c
    lane = iota((FACE, 128), 1)
    j3[...] = jnp.zeros_like(j3)

    for load in loads[0:9]:
        load.wait()
    mask = jnp.where(c == 0, 1.0, mask_i[...].astype(F32))

    def mask_start(layer, carry):
        put(start, layer, get(start, layer) * mask)
        return carry

    lax.fori_loop(0, LEV, mask_start, 0)

    def surface_trace(ref):
        return jnp.where(c == 0, c_trace(ref, 0, surface), c_trace(ref, 1, surface))

    def pack_block(block, dst):
        for q in range(4):
            dst[q, 0:40] = block[40 * (q % 2) : 40 * (q % 2) + 40, 128 * (q // 2) : 128 * (q // 2) + 128]

    def pack_rims(ref, dst):
        east = west = far = near = jnp.zeros((FACE, 128), F32)
        for layer in range(LEV):
            for half in range(2):
                v = ref[2 * layer + half]
                here = lane // 16 == layer
                if half == 1:
                    east = jnp.where(here, pltpu.roll(a_trace(v, 1), (16 * layer + 16) % 128, 1), east)
                else:
                    west = jnp.where(here, pltpu.roll(a_trace(v, 0), 16 * layer, 1), west)
                there = lane % 16 == layer + 4 * half
                far = jnp.where(there, pltpu.roll(b_trace(v, 1), (layer + 4 * half + 113) % 128, 1), far)
                near = jnp.where(there, pltpu.roll(b_trace(v, 0), layer + 4 * half, 1), near)
        dst[0, 0:40], dst[1, 0:40] = fold_half(east, 64), fold_half(west, 64)
        dst[2, 0:40], dst[3, 0:40] = fold_half(far, 8), fold_half(near, 8)

    count = [0]

    def remote(src, dst, device):
        k = count[0]
        count[0] += 1
        return pltpu.make_async_remote_copy(
            src_ref=src, dst_ref=dst, send_sem=send_sem.at[k], recv_sem=recv_sem.at[k],
            device_id=device, device_id_type=MESH,
        )

    own = surface_trace(start)
    pack_block(own, s1)
    pack_rims(start, rim_out.at[0])
    rim_out[0, 0, 40:48] = jnp.broadcast_to(pltpu.roll(mask[:, 128:256], 16, 1), (8, 128))
    rim_out[0, 1, 40:48] = jnp.broadcast_to(mask[:, 0:128], (8, 128))
    side_out[0] = fold_x(pltpu.roll(own[:, 128:256], 16, 1))
    side_out[1] = fold_x(own[:, 0:128])

    loads[12].wait()

    off = inter[y]
    delta = jnp.where(c == 0, off, 8 - off) % 8
    shift = delta % 4
    z_from = (g + delta) % 8 // 4
    z_pick = jnp.where(z_from == z, 0, 1)

    swap_face = remote(face_out, face_in, mates[0][2])
    copies1 = [remote(s1.at[q], r1.at[q], phase1[q]) for q in range(4)]
    copies2 = [remote(s2.at[d], r2.at[zf, d], dev) for zf, d, dev in phase2]
    uas = [remote(ua_out.at[d], ua_in.at[zf, d], dev) for zf, d, dev in mates]
    ubs = [remote(ub_out.at[d], ub_in.at[d], place(c, z, x + d)) for d in range(1, 4)]
    patches = [remote(patch_out, patch_in.at[zf, d], dev) for zf, d, dev in mates]
    around = [
        {"comp": c, "gx": (g + 1) % 8, "gy": y},
        {"comp": c, "gx": (g + 7) % 8, "gy": y},
        north,
        south,
    ]
    rims = [
        [remote(rim_out.at[m, k, part], rim_in.at[m, k, part], around[k])
         for k, part in enumerate([pl.ds(0, 48)] * 2 + [pl.ds(0, 40)] * 2)]
        for m in range(2)
    ]
    edges = [remote(edge_out.at[k], edge_in.at[k], around[k]) for k in range(4)]
    sides = []
    base = count[0]
    for k in range(2):
        for zz in range(2):
            n = 2 * k + zz
            sides.append(pltpu.make_async_remote_copy(
                src_ref=side_out.at[k], dst_ref=side_in.at[g], send_sem=send_sem.at[base + n],
                recv_sem=side_sem.at[g], device_id=place(other, zz, 3 * k), device_id_type=MESH,
            ))
    sides_in = [
        pltpu.make_async_remote_copy(
            src_ref=side_out.at[0], dst_ref=side_in.at[i], send_sem=send_sem.at[base],
            recv_sem=side_sem.at[i], device_id=mates[0][2], device_id_type=MESH,
        )
        for i in range(8)
    ]
    has = [x < 3, x > 0, y < last_y, y > 0]
    gets = [x > 0, x < 3, y > 0, y < last_y]

    def start_rims(m):
        rims[m][0].start()
        rims[m][1].start()
        for k in (2, 3):
            pl.when(has[k])(rims[m][k].start)

    def wait_rims(m):
        rims[m][0].wait_recv()
        rims[m][1].wait_recv()
        for k in (2, 3):
            pl.when(gets[k])(rims[m][k].wait_recv)

            @pl.when(jnp.logical_not(gets[k]))
            def _():
                rim_in[m, k] = jnp.zeros((48, 128), F32)

    def forward():
        for copy in copies1:
            copy.wait_recv()
        for d in range(4):
            s2[d] = r1[(8 - d - shift) % 4]
        for copy in copies2:
            copy.start()
        r2[0, 0] = s2[0]

    def joined(q):
        left = jnp.concatenate([q[0][0:40], q[1][0:40]], axis=0)
        right = jnp.concatenate([q[2][0:40], q[3][0:40]], axis=0)
        return jnp.concatenate([left, right], axis=1)

    def collect():
        for copy in copies2:
            copy.wait_recv()
        return joined([r2[z_pick, (8 - i - shift) % 4] for i in range(4)])

    def forward_base():
        for copy in uas:
            copy.wait_recv()
        for d in range(4):
            z_of = (z * 4 + (x + d) % 4 + delta) % 8 // 4
            ub_out[d] = ua_in[jnp.where(z_of == z, 0, 1), (8 - d - shift) % 4]
        for copy in ubs:
            copy.start()
        ub_in[0] = ub_out[0]

    wide = iota((FACE, COLS), 1)

    def local(src, layer):
        lanes = layer_lanes(layer)
        v = get(src, layer)
        j3[0:SLOT] = split3(
            jnp.where(wide < 16, 0.0, pltpu.roll(a_trace(v, 1), 16, 1)) - a_trace(v, 0)
        )
        j3[SLOT : 2 * SLOT] = split3(
            jnp.where(wide >= 240, 0.0, pltpu.roll(a_trace(v, 0), 240, 1)) - a_trace(v, 1)
        )
        low, high = b_trace(v, 0), b_trace(v, 1)
        j3[2 * SLOT : 3 * SLOT] = split3(jnp.where(wide % 16 == 0, 0.0, pltpu.roll(high, 1, 1)) - low)
        j3[3 * SLOT : 4 * SLOT] = split3(jnp.where(wide % 16 == 15, 0.0, pltpu.roll(low, 255, 1)) - high)
        below = c_trace(src, 1, jnp.maximum(layer - 1, 0))
        above = c_trace(src, 0, jnp.minimum(layer + 1, LEV - 1))
        j3[4 * SLOT : 5 * SLOT] = split3(jnp.where(layer > 0, below, 0.0) - c_trace(src, 0, layer))
        j3[5 * SLOT :] = split3(jnp.where(layer < LEV - 1, above, 0.0) - c_trace(src, 1, layer))
        lifted = jnp.dot(lift[...], j3[...], preferred_element_type=F32)
        term = jnp.dot(volume[...], v.astype(BF16), preferred_element_type=F32)
        weight = STEP * metric[:, lanes]
        term = (term.reshape(5, 64, COLS) * weight[None]).reshape(ROWS, COLS)
        return (term + lifted) * mask

    def lift_rims(rims):
        upper = iota((FACE, 128), 0) % 8 >= 4
        for k in range(4):
            r = jnp.dot(small[k], split3(rims[k]), preferred_element_type=F32)
            terms[k] = r
            if k == 2:
                terms[4] = jnp.where(upper, 0.0, r)
                terms[5] = jnp.where(upper, 0.0, pltpu.roll(r, FACE - 4, 0))
            if k == 3:
                terms[6] = jnp.where(upper, pltpu.roll(r, 4, 0), 0.0)
                terms[7] = jnp.where(upper, r, 0.0)

    def spread_rims(half, to_x, to_near, to_far):
        if half == 0:
            side = jnp.where(lane < 16, pltpu.roll(terms[0], to_x, 1), 0.0)
        else:
            side = jnp.where(lane >= 112, pltpu.roll(terms[1], to_x, 1), 0.0)
        near = [jnp.where(lane % 16 == 0, pltpu.roll(terms[4 + i], to_near, 1), 0.0) for i in range(2)]
        far = [jnp.where(lane % 16 == 15, pltpu.roll(terms[6 + i], to_far, 1), 0.0) for i in range(2)]
        tiles = []
        for r in range(10):
            for i in range(2):
                for k in range(2):
                    tile = (far if k else near)[i][8 * r : 8 * r + 8]
                    if r % 2 == half and i == half:
                        tile = tile + side[r // 2 * 16 + 8 * k : r // 2 * 16 + 8 * k + 8]
                    tiles.append(tile)
        return jnp.concatenate(tiles, axis=0) * mask[:, 128 * half : 128 * half + 128]

    def layer_rims(half, layer):
        step = layer + 4 * half
        to_x = (128 - 16 * layer) % 128 if half == 0 else 112 - 16 * layer
        return spread_rims(half, to_x, (128 - step) % 128, (143 - step) % 128)

    def unfold_rims(m):
        return [unfold_half(rim_in[m, k, 0:40], 64 if k < 2 else 8) for k in range(4)]

    def interface_part(block):
        op = lift[:, pl.ds(pl.multiple_of((4 + c) * SLOT, SLOT), SLOT)]
        return jnp.dot(op, split3(block), preferred_element_type=F32) * mask

    def first(layer):
        put(w, layer, get(start, layer) + local(start, layer))

    def prepare():
        for load in loads[9:12]:
            load.wait()
        row = iota((FACE, SLOT), 0)
        col = iota((FACE, SLOT), 1)
        to_high = ((col == row) | (col == row + FACE)).astype(BF16)
        to_low = (col == row + 2 * FACE).astype(BF16)
        for face in range(6):
            scaled = STEP * faces[face]
            high = scaled.astype(BF16)
            low = (scaled - high.astype(F32)).astype(BF16)
            spread = jnp.dot(high, to_high, preferred_element_type=F32) + jnp.dot(
                low, to_low, preferred_element_type=F32
            )
            small[face] = spread.astype(BF16)
            lift[:, face * SLOT : face * SLOT + SLOT] = jnp.dot(
                placement(face), small[face], preferred_element_type=F32
            ).astype(BF16)
        face_out[...] = small[4 + c].astype(F32)

        first(surface)
        held = surface_trace(w)
        pack_block(held, ua_out)
        for q in range(4):
            ua_out[q, 40:48] = jnp.broadcast_to(mask[:, 128 * (q // 2) : 128 * (q // 2) + 128], (8, 128))

    pl.semaphore_wait(
        barrier, 15 + jnp.where(y < last_y, 1, 0) + jnp.where(y > 0, 1, 0)
    )

    start_rims(0)
    for copy in copies1 + sides:
        copy.start()

    prepare()

    for copy in uas + [swap_face]:
        copy.start()

    def others(step):
        def run(i, carry):
            step(i + 1 - c)
            return carry

        lax.fori_loop(0, LEV - 1, run, 0)

    others(first)
    forward()

    wait_rims(0)
    lift_rims(unfold_rims(0))
    def first_rims(layer, carry):
        for half in range(2):
            w[2 * layer + half] = w[2 * layer + half] + layer_rims(half, layer)
        return carry

    lax.fori_loop(0, LEV, first_rims, 0)
    pack_rims(w, rim_out.at[1])
    start_rims(1)

    for k in range(4):
        patch_rows[FACE * k : FACE * k + FACE] = terms[k]
    nodes = jnp.where(
        c == 0, patch_rows[pl.ds(0, FACE, stride=4), :], patch_rows[pl.ds(3, FACE, stride=4), :]
    )
    on_x = pltpu.roll(nodes[0:40], (128 - 48 * c) % 128, 1)
    on_y = jnp.where(
        iota((40, 128), 1) % 16 == 0,
        pltpu.roll(nodes[40:80], (128 - 3 * c) % 128, 1),
        pltpu.roll(nodes[40:80], 125 - 3 * c, 1),
    )
    lane8 = iota((8, 128), 1)
    folded = [jnp.zeros((8, 128), F32)] * 2
    for r in range(5):
        tile = on_x[8 * r : 8 * r + 8]
        folded[0] = jnp.where(lane8 // 16 == r, pltpu.roll(tile, 16 * r, 1), folded[0])
        tile = on_y[8 * r : 8 * r + 8]
        folded[1] = jnp.where(lane8 % 16 // 2 == r, pltpu.roll(tile, 2 * r, 1), folded[1])
    patch_out[...] = jnp.concatenate(folded, axis=0)
    for copy in patches:
        copy.start()

    swap_face.wait_recv()
    reply = jnp.dot(face_in[...].astype(BF16), split3(surface_trace(start)), preferred_element_type=F32)

    def second(layer):
        acc[:, layer_lanes(layer)] = get(start, layer) + get(w, layer) + local(w, layer)

    others(second)
    forward_base()

    put(w, surface, get(w, surface) + interface_part(collect()))

    v0, v1 = w[2 * surface], w[2 * surface + 1]
    first_two = lane % 16 == 0
    edge_out[0] = fold_x(pltpu.roll(a_trace(v1, 1), 16, 1))
    edge_out[1] = fold_x(a_trace(v0, 0))
    edge_out[2] = fold_y(
        jnp.where(first_two, pltpu.roll(b_trace(v0, 1), 113, 1), pltpu.roll(b_trace(v1, 1), 114, 1))
    )
    edge_out[3] = fold_y(jnp.where(first_two, b_trace(v0, 0), pltpu.roll(b_trace(v1, 0), 1, 1)))
    for k in range(4):
        pl.when(has[k])(edges[k].start)

    second(surface)
    wait_rims(1)
    lift_rims(unfold_rims(1))

    def second_rims(layer):
        part = jnp.concatenate([layer_rims(0, layer), layer_rims(1, layer)], axis=1)
        lanes = layer_lanes(layer)
        acc[:, lanes] = 0.5 * (acc[:, lanes] + part)

    others(second_rims)

    for copy in ubs + patches:
        copy.wait_recv()
    q = [ub_in[(8 - i - shift) % 4] for i in range(4)]
    wet = jnp.concatenate([q[0][40:41], q[2][40:41]], axis=1)
    patch = patch_in[z_pick, (4 - shift) % 4]
    tiles = [pltpu.roll(patch[0:8], (128 - 16 * r) % 128, 1) for r in range(5)]
    tiles += [pltpu.roll(patch[8:16], (128 - 2 * r) % 128, 1) for r in range(5)]
    packed = jnp.concatenate(tiles, axis=0)
    high = packed.astype(BF16)
    low = (packed - high.astype(F32)).astype(BF16)
    row = iota((2 * FACE, FACE), 0)
    col = iota((2 * FACE, FACE), 1)
    node, face, index = row % FACE, col // 20, col % 20
    target = index // 4 * 16 + jnp.where(face < 2, index % 4 + 12 * face, index % 4 * 4 + 3 * (face - 2))
    to_node = ((node == target) & (row // FACE == face // 2)).astype(BF16)
    spread = jnp.dot(to_node, high, preferred_element_type=F32) + jnp.dot(
        to_node, low, preferred_element_type=F32
    )
    on_x, on_y = spread[0:FACE], spread[FACE:]
    node = iota((FACE, 128), 0)
    node_a, node_b = node // 4 % 4, node % 4
    halves = []
    for h in range(2):
        side = (
            jnp.where((lane < 16) & (node_a == 0), on_x, 0.0)
            if h == 0
            else jnp.where((lane >= 112) & (node_a == 3), pltpu.roll(on_x, 112, 1), 0.0)
        )
        near = jnp.where((lane % 16 == 0) & (node_b == 0), pltpu.roll(on_y, (128 - h) % 128, 1), 0.0)
        far = jnp.where((lane % 16 == 15) & (node_b == 3), pltpu.roll(on_y, 15 - h, 1), 0.0)
        halves.append(side + near + far)
    block = joined(q) + wet * (jnp.concatenate(halves, axis=1) + reply)
    lanes = layer_lanes(surface)
    acc[:, lanes] = 0.5 * (acc[:, lanes] + interface_part(block))

    def finish_edge(k):
        for copy in sides_in:
            copy.wait_recv()
        partner = (g + (7 if k == 0 else 1) + delta) % 8
        row = iota((FACE, FACE), 0)
        col = iota((FACE, FACE), 1)
        pick = (
            (row // 16 == col // 16) & (row % 4 == 3 * c) & (col % 4 == row // 4 % 4)
            & (col // 4 % 4 == (3 if k == 0 else 0))
        ).astype(BF16)
        op = jnp.dot(pick, small[4 + c], preferred_element_type=F32).astype(BF16)
        term = jnp.dot(op, split3(unfold_x(side_in[partner])), preferred_element_type=F32)
        held = pltpu.roll(unfold_half(rim_in[1, k, 0:40], 64), (128 - 48 * c) % 128, 1)
        rim_edge[k] = held + term * rim_in[0, k, 40:41]

    def take_edge(k):
        edges[k].wait_recv()
        rim_edge[k] = unfold_x(edge_in[k]) if k < 2 else unfold_y(edge_in[k])

    for k in range(4):
        pl.when(gets[k])(functools.partial(take_edge, k))

        @pl.when(jnp.logical_not(gets[k]))
        def _():
            if k < 2:
                finish_edge(k)
            else:
                rim_edge[k] = jnp.zeros((FACE, 128), F32)

    lift_rims([rim_edge[k] for k in range(4)])
    part = jnp.concatenate(
        [spread_rims(0, 0, 0, 15), spread_rims(1, 112, 127, 14)], axis=1
    )
    acc[:, lanes] = acc[:, lanes] + 0.5 * part

    for copy in [swap_face] + copies1 + copies2 + uas + ubs + patches + sides:
        copy.wait_send()
    for m in range(2):
        rims[m][0].wait_send()
        rims[m][1].wait_send()
        for k in (2, 3):
            pl.when(has[k])(rims[m][k].wait_send)
    for k in range(4):
        pl.when(has[k])(edges[k].wait_send)


def body(cotangent, metric, volume_ops, face_ops, land_mask, intersection):
    copies = 47
    out = pl.pallas_call(
        kernel,
        out_shape=jax.ShapeDtypeStruct((ROWS, LEV * COLS), F32),
        in_specs=[pl.BlockSpec(memory_space=pltpu.HBM)] * 6,
        out_specs=pl.BlockSpec(memory_space=pltpu.VMEM),
        scratch_shapes=[
            pltpu.SMEM((16,), jnp.int32),
            pltpu.VMEM((2 * LEV, ROWS, 128), F32),
            pltpu.VMEM((64, LEV * COLS), F32),
            pltpu.VMEM((ROWS, ROWS), BF16),
            pltpu.VMEM((6, FACE, FACE), F32),
            pltpu.VMEM((1, COLS), jnp.int32),
            pltpu.VMEM((2 * LEV, ROWS, 128), F32),
            pltpu.VMEM((ROWS, 6 * SLOT), BF16),
            pltpu.VMEM((6, FACE, SLOT), BF16),
            pltpu.VMEM((6 * SLOT, COLS), BF16),
            pltpu.VMEM((FACE, SLOT), F32),
            pltpu.VMEM((FACE, SLOT), F32),
            pltpu.VMEM((2, 4, 48, 128), F32),
            pltpu.VMEM((2, 4, 48, 128), F32),
            pltpu.VMEM((4, 40, 128), F32),
            pltpu.VMEM((4, 40, 128), F32),
            pltpu.VMEM((4, 40, 128), F32),
            pltpu.VMEM((2, 4, 40, 128), F32),
            pltpu.VMEM((4, 48, 128), F32),
            pltpu.VMEM((2, 4, 48, 128), F32),
            pltpu.VMEM((4, 48, 128), F32),
            pltpu.VMEM((4, 48, 128), F32),
            pltpu.VMEM((ROWS, 128), F32),
            pltpu.VMEM((16, 128), F32),
            pltpu.VMEM((2, 4, 16, 128), F32),
            pltpu.VMEM((2, 16, 128), F32),
            pltpu.VMEM((8, 16, 128), F32),
            pltpu.VMEM((4, 16, 128), F32),
            pltpu.VMEM((4, 16, 128), F32),
            pltpu.VMEM((4, FACE, 128), F32),
            pltpu.VMEM((8, FACE, 128), F32),
            pltpu.SemaphoreType.DMA((13,)),
            pltpu.SemaphoreType.DMA((copies,)),
            pltpu.SemaphoreType.DMA((copies,)),
            pltpu.SemaphoreType.DMA((8,)),
        ],
        compiler_params=pltpu.CompilerParams(
            collective_id=0, has_side_effects=True, vmem_limit_bytes=48 * 1024 * 1024
        ),
    )(
        *(
            pltpu.with_memory_space_constraint(a, pltpu.HBM)
            for a in (
                intersection,
                cotangent[0, 0, 0],
                metric[0, 0, 0],
                volume_ops[0],
                face_ops[0],
                land_mask[0],
            )
        )
    )
    return out[None, None, None]


def solution(mesh):
    in_specs = (
        P("comp", "gx", "gy", None, None),
        P("comp", "gx", "gy", None, None),
        P("comp", None, None),
        P("comp", None, None, None),
        P("gx", "gy", None),
        P(),
    )
    out_specs = P("comp", "gx", "gy", None, None)
    return jax.shard_map(body, mesh=mesh, in_specs=in_specs, out_specs=out_specs, check_vma=False)
```

```python
import functools

import jax
import jax.numpy as jnp
from jax import lax
from jax.experimental import pallas as pl
from jax.experimental.pallas import tpu as pltpu
from jax.sharding import PartitionSpec as P

MESH = pl.DeviceIdType.MESH
F32 = jnp.float32
BF16 = jnp.bfloat16
ROWS = 320
COLS = 256
LEV = 4
FACE = 80
SLOT = 256
STEP = 0.4


def iota(shape, axis):
    return lax.broadcasted_iota(jnp.int32, shape, axis)


def split3(x):
    high = x.astype(BF16)
    low = (x - high.astype(F32)).astype(BF16)
    return jnp.concatenate([high, low, high, jnp.zeros((16, x.shape[1]), BF16)], axis=0)


def a_trace(v, pos):
    n = v.shape[-1]
    return v.reshape(5, 64, n)[:, 48 * pos : 48 * pos + 16].reshape(FACE, n)


def b_trace(v, pos):
    n = v.shape[-1]
    tiles = v.reshape(10, 2, 2, 8, n)
    even = tiles[:, 0, pos].reshape(FACE, n)
    odd = tiles[:, 1, pos].reshape(FACE, n)
    lower = iota((FACE, n), 0) % 8 < 4
    if pos == 0:
        return jnp.where(lower, even, pltpu.roll(odd, 4, 0))
    return jnp.where(lower, pltpu.roll(even, FACE - 4, 0), odd)


def c_trace(ref, pos, layer):
    rows = pl.ds(3 * pos, FACE, stride=4)
    return jnp.concatenate([ref[2 * layer, rows, :], ref[2 * layer + 1, rows, :]], axis=1)


def get(ref, layer):
    return jnp.concatenate([ref[2 * layer], ref[2 * layer + 1]], axis=1)


def put(ref, layer, value):
    ref[2 * layer] = value[:, 0:128]
    ref[2 * layer + 1] = value[:, 128:256]


def placement(face):
    row = iota((ROWS, FACE), 0)
    col = iota((1, FACE), 1)
    field, first, second = col // 16, col // 4 % 4, col % 4
    pos = 3 * (face % 2)
    if face // 2 == 0:
        node = pos * 16 + first * 4 + second
    elif face // 2 == 1:
        node = first * 16 + pos * 4 + second
    else:
        node = first * 16 + second * 4 + pos
    return (row == field * 64 + node).astype(BF16)


def fold_x(v):
    lane = iota((8, 128), 1)
    out = [jnp.zeros((8, 128), F32)] * 2
    for r in range(10):
        j = r % 8
        out[r // 8] = jnp.where(lane // 16 == j, pltpu.roll(v[8 * r : 8 * r + 8], 16 * j, 1), out[r // 8])
    return jnp.concatenate(out, axis=0)


def unfold_x(v):
    tiles = []
    for r in range(10):
        part = v[r // 8 * 8 : r // 8 * 8 + 8]
        tiles.append(pltpu.roll(part, (128 - 16 * (r % 8)) % 128, 1))
    return jnp.concatenate(tiles, axis=0)


def fold_y(v):
    lane = iota((8, 128), 1)
    out = [jnp.zeros((8, 128), F32)] * 2
    for r in range(10):
        j = r % 8
        out[r // 8] = jnp.where(lane % 16 // 2 == j, pltpu.roll(v[8 * r : 8 * r + 8], 2 * j, 1), out[r // 8])
    return jnp.concatenate(out, axis=0)


def unfold_y(v):
    tiles = []
    for r in range(10):
        part = v[r // 8 * 8 : r // 8 * 8 + 8]
        tiles.append(pltpu.roll(part, (128 - 2 * (r % 8)) % 128, 1))
    return jnp.concatenate(tiles, axis=0)


def fold_half(v, by):
    lane = iota((40, 128), 1)
    return jnp.where(lane % (2 * by) < by, v[0:40], pltpu.roll(v[40:80], by, 1))


def unfold_half(v, by):
    return jnp.concatenate([v, pltpu.roll(v, 128 - by, 1)], axis=0)


def layer_lanes(layer):
    return pl.ds(pl.multiple_of(layer * COLS, COLS), COLS)


def kernel(
    inter_hbm, cot_hbm, metric_hbm, volume_hbm, face_hbm, mask_hbm, acc,
    inter, start, metric, volume, faces, mask_i,
    w, lift, small, j3, face_out, face_in,
    rim_out, rim_in, s1, r1, s2, r2, ua_out, ua_in, ub_out, ub_in,
    patch_rows, patch_out, patch_in, side_out, side_in, edge_out, edge_in, rim_edge, terms,
    local_sem, send_sem, recv_sem, side_sem,
):
    c = lax.axis_index("comp")
    g = lax.axis_index("gx")
    y = lax.axis_index("gy")
    z, x = g // 4, g % 4
    last_y = lax.axis_size("gy") - 1
    other = 1 - c

    def place(comp, zz, xx):
        return {"comp": comp, "gx": zz * 4 + xx % 4, "gy": y}

    mates = [(zf, d, place(other, (z + zf) % 2, x + d)) for zf in range(2) for d in range(4)]
    phase1 = [place(other, z, x + q) for q in range(4)]
    phase2 = [(zf, d, place(c, (z + zf) % 2, x + d)) for zf in range(2) for d in range(4) if zf or d]
    north = {"comp": c, "gx": g, "gy": jnp.minimum(y + 1, last_y)}
    south = {"comp": c, "gx": g, "gy": jnp.maximum(y - 1, 0)}

    barrier = pltpu.get_barrier_semaphore()
    for device in [d for _, _, d in mates + phase2]:
        pl.semaphore_signal(barrier, inc=1, device_id=device, device_id_type=MESH)

    @pl.when(y < last_y)
    def _():
        pl.semaphore_signal(barrier, inc=1, device_id=north, device_id_type=MESH)

    @pl.when(y > 0)
    def _():
        pl.semaphore_signal(barrier, inc=1, device_id=south, device_id_type=MESH)

    loads = [
        pltpu.make_async_copy(src, dst, local_sem.at[i])
        for i, (src, dst) in enumerate(
            [(cot_hbm.at[:, 128 * t : 128 * t + 128], start.at[t]) for t in range(8)]
            + [
                (mask_hbm, mask_i),
                (face_hbm, faces),
                (volume_hbm, volume),
                (metric_hbm, metric),
                (inter_hbm, inter),
            ]
        )
    ]
    for load in loads:
        load.start()

    surface = 3 * c
    lane = iota((FACE, 128), 1)
    j3[...] = jnp.zeros_like(j3)

    for load in loads[0:9]:
        load.wait()
    mask = jnp.where(c == 0, 1.0, mask_i[...].astype(F32))

    def mask_start(layer, carry):
        put(start, layer, get(start, layer) * mask)
        return carry

    lax.fori_loop(0, LEV, mask_start, 0)

    def surface_trace(ref):
        return jnp.where(c == 0, c_trace(ref, 0, surface), c_trace(ref, 1, surface))

    def pack_block(block, dst):
        for q in range(4):
            dst[q, 0:40] = block[40 * (q % 2) : 40 * (q % 2) + 40, 128 * (q // 2) : 128 * (q // 2) + 128]

    def pack_rims(ref, dst):
        east = west = far = near = jnp.zeros((FACE, 128), F32)
        for layer in range(LEV):
            for half in range(2):
                v = ref[2 * layer + half]
                here = lane // 16 == layer
                if half == 1:
                    east = jnp.where(here, pltpu.roll(a_trace(v, 1), (16 * layer + 16) % 128, 1), east)
                else:
                    west = jnp.where(here, pltpu.roll(a_trace(v, 0), 16 * layer, 1), west)
                there = lane % 16 == layer + 4 * half
                far = jnp.where(there, pltpu.roll(b_trace(v, 1), (layer + 4 * half + 113) % 128, 1), far)
                near = jnp.where(there, pltpu.roll(b_trace(v, 0), layer + 4 * half, 1), near)
        dst[0, 0:40], dst[1, 0:40] = fold_half(east, 64), fold_half(west, 64)
        dst[2, 0:40], dst[3, 0:40] = fold_half(far, 8), fold_half(near, 8)

    count = [0]

    def remote(src, dst, device):
        k = count[0]
        count[0] += 1
        return pltpu.make_async_remote_copy(
            src_ref=src, dst_ref=dst, send_sem=send_sem.at[k], recv_sem=recv_sem.at[k],
            device_id=device, device_id_type=MESH,
        )

    own = surface_trace(start)
    pack_block(own, s1)
    pack_rims(start, rim_out.at[0])
    rim_out[0, 0, 40:48] = jnp.broadcast_to(pltpu.roll(mask[:, 128:256], 16, 1), (8, 128))
    rim_out[0, 1, 40:48] = jnp.broadcast_to(mask[:, 0:128], (8, 128))
    side_out[0] = fold_x(pltpu.roll(own[:, 128:256], 16, 1))
    side_out[1] = fold_x(own[:, 0:128])

    loads[12].wait()

    off = inter[y]
    delta = jnp.where(c == 0, off, 8 - off) % 8
    shift = delta % 4
    z_from = (g + delta) % 8 // 4
    z_pick = jnp.where(z_from == z, 0, 1)

    swap_face = remote(face_out, face_in, mates[0][2])
    copies1 = [remote(s1.at[q], r1.at[q], phase1[q]) for q in range(4)]
    copies2 = [remote(s2.at[d], r2.at[zf, d], dev) for zf, d, dev in phase2]
    uas = [
        remote(ua_out.at[d, pl.ds(0, 40 if d else 48)], ua_in.at[zf, d, pl.ds(0, 40 if d else 48)], dev)
        for zf, d, dev in mates
    ]
    ubs = [remote(ub_out.at[d], ub_in.at[d], place(c, z, x + d)) for d in range(1, 4)]
    patches = [remote(patch_out, patch_in.at[zf, d], dev) for zf, d, dev in mates]
    around = [
        {"comp": c, "gx": (g + 1) % 8, "gy": y},
        {"comp": c, "gx": (g + 7) % 8, "gy": y},
        north,
        south,
    ]
    rims = [
        [remote(rim_out.at[m, k, part], rim_in.at[m, k, part], around[k])
         for k, part in enumerate([pl.ds(0, 48)] * 2 + [pl.ds(0, 40)] * 2)]
        for m in range(2)
    ]
    edges = [remote(edge_out.at[k], edge_in.at[k], around[k]) for k in range(4)]
    sides = []
    base = count[0]
    for k in range(2):
        for zz in range(2):
            n = 2 * k + zz
            sides.append(pltpu.make_async_remote_copy(
                src_ref=side_out.at[k], dst_ref=side_in.at[g], send_sem=send_sem.at[base + n],
                recv_sem=side_sem.at[g], device_id=place(other, zz, 3 * k), device_id_type=MESH,
            ))
    sides_in = [
        pltpu.make_async_remote_copy(
            src_ref=side_out.at[0], dst_ref=side_in.at[i], send_sem=send_sem.at[base],
            recv_sem=side_sem.at[i], device_id=mates[0][2], device_id_type=MESH,
        )
        for i in range(8)
    ]
    has = [x < 3, x > 0, y < last_y, y > 0]
    gets = [x > 0, x < 3, y > 0, y < last_y]

    def start_rims(m):
        rims[m][0].start()
        rims[m][1].start()
        for k in (2, 3):
            pl.when(has[k])(rims[m][k].start)

    def wait_rims(m):
        rims[m][0].wait_recv()
        rims[m][1].wait_recv()
        for k in (2, 3):
            pl.when(gets[k])(rims[m][k].wait_recv)

            @pl.when(jnp.logical_not(gets[k]))
            def _():
                rim_in[m, k] = jnp.zeros((48, 128), F32)

    def forward():
        for copy in copies1:
            copy.wait_recv()
        for d in range(4):
            s2[d] = r1[(8 - d - shift) % 4]
        for copy in copies2[3:] + copies2[:3]:
            copy.start()
        r2[0, 0] = s2[0]

    def joined(q):
        left = jnp.concatenate([q[0][0:40], q[1][0:40]], axis=0)
        right = jnp.concatenate([q[2][0:40], q[3][0:40]], axis=0)
        return jnp.concatenate([left, right], axis=1)

    def collect():
        for copy in copies2:
            copy.wait_recv()
        return joined([r2[z_pick, (8 - i - shift) % 4] for i in range(4)])

    def forward_base():
        for copy in uas:
            copy.wait_recv()
        for d in range(4):
            z_of = (z * 4 + (x + d) % 4 + delta) % 8 // 4
            ub_out[d] = ua_in[jnp.where(z_of == z, 0, 1), (8 - d - shift) % 4]
        for copy in ubs:
            copy.start()
        ub_in[0] = ub_out[0]

    wide = iota((FACE, COLS), 1)

    def local(src, layer):
        lanes = layer_lanes(layer)
        v = get(src, layer)
        j3[0:SLOT] = split3(
            jnp.where(wide < 16, 0.0, pltpu.roll(a_trace(v, 1), 16, 1)) - a_trace(v, 0)
        )
        j3[SLOT : 2 * SLOT] = split3(
            jnp.where(wide >= 240, 0.0, pltpu.roll(a_trace(v, 0), 240, 1)) - a_trace(v, 1)
        )
        low, high = b_trace(v, 0), b_trace(v, 1)
        j3[2 * SLOT : 3 * SLOT] = split3(jnp.where(wide % 16 == 0, 0.0, pltpu.roll(high, 1, 1)) - low)
        j3[3 * SLOT : 4 * SLOT] = split3(jnp.where(wide % 16 == 15, 0.0, pltpu.roll(low, 255, 1)) - high)
        below = c_trace(src, 1, jnp.maximum(layer - 1, 0))
        above = c_trace(src, 0, jnp.minimum(layer + 1, LEV - 1))
        j3[4 * SLOT : 5 * SLOT] = split3(jnp.where(layer > 0, below, 0.0) - c_trace(src, 0, layer))
        j3[5 * SLOT :] = split3(jnp.where(layer < LEV - 1, above, 0.0) - c_trace(src, 1, layer))
        lifted = jnp.dot(lift[...], j3[...], preferred_element_type=F32)
        term = jnp.dot(volume[...], v.astype(BF16), preferred_element_type=F32)
        weight = STEP * metric[:, lanes]
        term = (term.reshape(5, 64, COLS) * weight[None]).reshape(ROWS, COLS)
        return (term + lifted) * mask

    def lift_rims(rims):
        upper = iota((FACE, 128), 0) % 8 >= 4
        for k in range(4):
            r = jnp.dot(small[k], split3(rims[k]), preferred_element_type=F32)
            terms[k] = r
            if k == 2:
                terms[4] = jnp.where(upper, 0.0, r)
                terms[5] = jnp.where(upper, 0.0, pltpu.roll(r, FACE - 4, 0))
            if k == 3:
                terms[6] = jnp.where(upper, pltpu.roll(r, 4, 0), 0.0)
                terms[7] = jnp.where(upper, r, 0.0)

    def spread_rims(half, to_x, to_near, to_far):
        if half == 0:
            side = jnp.where(lane < 16, pltpu.roll(terms[0], to_x, 1), 0.0)
        else:
            side = jnp.where(lane >= 112, pltpu.roll(terms[1], to_x, 1), 0.0)
        near = [jnp.where(lane % 16 == 0, pltpu.roll(terms[4 + i], to_near, 1), 0.0) for i in range(2)]
        far = [jnp.where(lane % 16 == 15, pltpu.roll(terms[6 + i], to_far, 1), 0.0) for i in range(2)]
        tiles = []
        for r in range(10):
            for i in range(2):
                for k in range(2):
                    tile = (far if k else near)[i][8 * r : 8 * r + 8]
                    if r % 2 == half and i == half:
                        tile = tile + side[r // 2 * 16 + 8 * k : r // 2 * 16 + 8 * k + 8]
                    tiles.append(tile)
        return jnp.concatenate(tiles, axis=0) * mask[:, 128 * half : 128 * half + 128]

    def layer_rims(half, layer):
        step = layer + 4 * half
        to_x = (128 - 16 * layer) % 128 if half == 0 else 112 - 16 * layer
        return spread_rims(half, to_x, (128 - step) % 128, (143 - step) % 128)

    def unfold_rims(m):
        return [unfold_half(rim_in[m, k, 0:40], 64 if k < 2 else 8) for k in range(4)]

    def interface_part(block):
        op = lift[:, pl.ds(pl.multiple_of((4 + c) * SLOT, SLOT), SLOT)]
        return jnp.dot(op, split3(block), preferred_element_type=F32) * mask

    def first(layer):
        put(w, layer, get(start, layer) + local(start, layer))

    def prepare():
        for load in loads[9:12]:
            load.wait()
        row = iota((FACE, SLOT), 0)
        col = iota((FACE, SLOT), 1)
        to_high = ((col == row) | (col == row + FACE)).astype(BF16)
        to_low = (col == row + 2 * FACE).astype(BF16)
        for face in range(6):
            scaled = STEP * faces[face]
            high = scaled.astype(BF16)
            low = (scaled - high.astype(F32)).astype(BF16)
            spread = jnp.dot(high, to_high, preferred_element_type=F32) + jnp.dot(
                low, to_low, preferred_element_type=F32
            )
            small[face] = spread.astype(BF16)
            lift[:, face * SLOT : face * SLOT + SLOT] = jnp.dot(
                placement(face), small[face], preferred_element_type=F32
            ).astype(BF16)
        face_out[...] = small[4 + c].astype(F32)

        first(surface)
        held = surface_trace(w)
        pack_block(held, ua_out)
        ua_out[0, 40:48] = jnp.where(
            iota((8, 128), 0) == 0,
            jnp.broadcast_to(mask[:, 0:128], (8, 128)),
            jnp.broadcast_to(mask[:, 128:256], (8, 128)),
        )

    pl.semaphore_wait(
        barrier, 15 + jnp.where(y < last_y, 1, 0) + jnp.where(y > 0, 1, 0)
    )

    start_rims(0)
    for copy in copies1 + sides:
        copy.start()

    prepare()

    for copy in uas[4:] + uas[:4] + [swap_face]:
        copy.start()

    def others(step):
        def run(i, carry):
            step(i + 1 - c)
            return carry

        lax.fori_loop(0, LEV - 1, run, 0)

    others(first)
    forward()

    wait_rims(0)
    lift_rims(unfold_rims(0))
    def first_rims(layer, carry):
        for half in range(2):
            w[2 * layer + half] = w[2 * layer + half] + layer_rims(half, layer)
        return carry

    lax.fori_loop(0, LEV, first_rims, 0)
    pack_rims(w, rim_out.at[1])
    start_rims(1)

    for k in range(4):
        patch_rows[FACE * k : FACE * k + FACE] = terms[k]
    nodes = jnp.where(
        c == 0, patch_rows[pl.ds(0, FACE, stride=4), :], patch_rows[pl.ds(3, FACE, stride=4), :]
    )
    on_x = pltpu.roll(nodes[0:40], (128 - 48 * c) % 128, 1)
    on_y = jnp.where(
        iota((40, 128), 1) % 16 == 0,
        pltpu.roll(nodes[40:80], (128 - 3 * c) % 128, 1),
        pltpu.roll(nodes[40:80], 125 - 3 * c, 1),
    )
    lane8 = iota((8, 128), 1)
    folded = [jnp.zeros((8, 128), F32)] * 2
    for r in range(5):
        tile = on_x[8 * r : 8 * r + 8]
        folded[0] = jnp.where(lane8 // 16 == r, pltpu.roll(tile, 16 * r, 1), folded[0])
        tile = on_y[8 * r : 8 * r + 8]
        folded[1] = jnp.where(lane8 % 16 // 2 == r, pltpu.roll(tile, 2 * r, 1), folded[1])
    patch_out[...] = jnp.concatenate(folded, axis=0)
    for copy in patches:
        copy.start()

    swap_face.wait_recv()
    reply = jnp.dot(face_in[...].astype(BF16), split3(surface_trace(start)), preferred_element_type=F32)

    def second(layer):
        acc[:, layer_lanes(layer)] = get(start, layer) + get(w, layer) + local(w, layer)

    others(second)
    forward_base()

    put(w, surface, get(w, surface) + interface_part(collect()))

    v0, v1 = w[2 * surface], w[2 * surface + 1]
    first_two = lane % 16 == 0
    edge_out[0] = fold_x(pltpu.roll(a_trace(v1, 1), 16, 1))
    edge_out[1] = fold_x(a_trace(v0, 0))
    edge_out[2] = fold_y(
        jnp.where(first_two, pltpu.roll(b_trace(v0, 1), 113, 1), pltpu.roll(b_trace(v1, 1), 114, 1))
    )
    edge_out[3] = fold_y(jnp.where(first_two, b_trace(v0, 0), pltpu.roll(b_trace(v1, 0), 1, 1)))
    for k in range(4):
        pl.when(has[k])(edges[k].start)

    second(surface)
    wait_rims(1)
    lift_rims(unfold_rims(1))

    def second_rims(layer):
        part = jnp.concatenate([layer_rims(0, layer), layer_rims(1, layer)], axis=1)
        lanes = layer_lanes(layer)
        acc[:, lanes] = 0.5 * (acc[:, lanes] + part)

    others(second_rims)

    for copy in ubs + patches:
        copy.wait_recv()
    q = [ub_in[(8 - i - shift) % 4] for i in range(4)]
    wet = jnp.concatenate([q[0][40:41], q[0][41:42]], axis=1)
    patch = patch_in[z_pick, (4 - shift) % 4]
    tiles = [pltpu.roll(patch[0:8], (128 - 16 * r) % 128, 1) for r in range(5)]
    tiles += [pltpu.roll(patch[8:16], (128 - 2 * r) % 128, 1) for r in range(5)]
    packed = jnp.concatenate(tiles, axis=0)
    high = packed.astype(BF16)
    low = (packed - high.astype(F32)).astype(BF16)
    row = iota((2 * FACE, FACE), 0)
    col = iota((1, FACE), 1)
    face, index = col // 20, col % 20
    target = index // 4 * 16 + jnp.where(face < 2, index % 4 + 12 * face, index % 4 * 4 + 3 * (face - 2))
    to_node = (row == target + FACE * (face // 2)).astype(BF16)
    spread = jnp.dot(to_node, high, preferred_element_type=F32) + jnp.dot(
        to_node, low, preferred_element_type=F32
    )
    on_x, on_y = spread[0:FACE], spread[FACE:]
    node = iota((FACE, 128), 0)
    node_a, node_b = node // 4 % 4, node % 4
    halves = []
    for h in range(2):
        side = (
            jnp.where((lane < 16) & (node_a == 0), on_x, 0.0)
            if h == 0
            else jnp.where((lane >= 112) & (node_a == 3), pltpu.roll(on_x, 112, 1), 0.0)
        )
        near = jnp.where((lane % 16 == 0) & (node_b == 0), pltpu.roll(on_y, (128 - h) % 128, 1), 0.0)
        far = jnp.where((lane % 16 == 15) & (node_b == 3), pltpu.roll(on_y, 15 - h, 1), 0.0)
        halves.append(side + near + far)
    block = joined(q) + wet * (jnp.concatenate(halves, axis=1) + reply)
    lanes = layer_lanes(surface)
    acc[:, lanes] = 0.5 * (acc[:, lanes] + interface_part(block))

    def finish_edge(k):
        for copy in sides_in:
            copy.wait_recv()
        partner = (g + (7 if k == 0 else 1) + delta) % 8
        row = iota((FACE, FACE), 0)
        col = iota((1, FACE), 1)
        target = jnp.where(col // 4 % 4 == (3 if k == 0 else 0), col // 16 * 16 + col % 4 * 4 + 3 * c, -1)
        pick = (row == target).astype(BF16)
        op = jnp.dot(pick, small[4 + c], preferred_element_type=F32).astype(BF16)
        term = jnp.dot(op, split3(unfold_x(side_in[partner])), preferred_element_type=F32)
        held = pltpu.roll(unfold_half(rim_in[1, k, 0:40], 64), (128 - 48 * c) % 128, 1)
        rim_edge[k] = held + term * rim_in[0, k, 40:41]

    def take_edge(k):
        edges[k].wait_recv()
        rim_edge[k] = unfold_x(edge_in[k]) if k < 2 else unfold_y(edge_in[k])

    for k in range(4):
        pl.when(gets[k])(functools.partial(take_edge, k))

        @pl.when(jnp.logical_not(gets[k]))
        def _():
            if k < 2:
                finish_edge(k)
            else:
                rim_edge[k] = jnp.zeros((FACE, 128), F32)

    lift_rims([rim_edge[k] for k in range(4)])
    part = jnp.concatenate(
        [spread_rims(0, 0, 0, 15), spread_rims(1, 112, 127, 14)], axis=1
    )
    acc[:, lanes] = acc[:, lanes] + 0.5 * part

    for copy in [swap_face] + copies1 + copies2 + uas + ubs + patches + sides:
        copy.wait_send()
    for m in range(2):
        rims[m][0].wait_send()
        rims[m][1].wait_send()
        for k in (2, 3):
            pl.when(has[k])(rims[m][k].wait_send)
    for k in range(4):
        pl.when(has[k])(edges[k].wait_send)


def body(cotangent, metric, volume_ops, face_ops, land_mask, intersection):
    copies = 47
    out = pl.pallas_call(
        kernel,
        out_shape=jax.ShapeDtypeStruct((ROWS, LEV * COLS), F32),
        in_specs=[pl.BlockSpec(memory_space=pltpu.HBM)] * 6,
        out_specs=pl.BlockSpec(memory_space=pltpu.VMEM),
        scratch_shapes=[
            pltpu.SMEM((16,), jnp.int32),
            pltpu.VMEM((2 * LEV, ROWS, 128), F32),
            pltpu.VMEM((64, LEV * COLS), F32),
            pltpu.VMEM((ROWS, ROWS), BF16),
            pltpu.VMEM((6, FACE, FACE), F32),
            pltpu.VMEM((1, COLS), jnp.int32),
            pltpu.VMEM((2 * LEV, ROWS, 128), F32),
            pltpu.VMEM((ROWS, 6 * SLOT), BF16),
            pltpu.VMEM((6, FACE, SLOT), BF16),
            pltpu.VMEM((6 * SLOT, COLS), BF16),
            pltpu.VMEM((FACE, SLOT), F32),
            pltpu.VMEM((FACE, SLOT), F32),
            pltpu.VMEM((2, 4, 48, 128), F32),
            pltpu.VMEM((2, 4, 48, 128), F32),
            pltpu.VMEM((4, 40, 128), F32),
            pltpu.VMEM((4, 40, 128), F32),
            pltpu.VMEM((4, 40, 128), F32),
            pltpu.VMEM((2, 4, 40, 128), F32),
            pltpu.VMEM((4, 48, 128), F32),
            pltpu.VMEM((2, 4, 48, 128), F32),
            pltpu.VMEM((4, 48, 128), F32),
            pltpu.VMEM((4, 48, 128), F32),
            pltpu.VMEM((ROWS, 128), F32),
            pltpu.VMEM((16, 128), F32),
            pltpu.VMEM((2, 4, 16, 128), F32),
            pltpu.VMEM((2, 16, 128), F32),
            pltpu.VMEM((8, 16, 128), F32),
            pltpu.VMEM((4, 16, 128), F32),
            pltpu.VMEM((4, 16, 128), F32),
            pltpu.VMEM((4, FACE, 128), F32),
            pltpu.VMEM((8, FACE, 128), F32),
            pltpu.SemaphoreType.DMA((13,)),
            pltpu.SemaphoreType.DMA((copies,)),
            pltpu.SemaphoreType.DMA((copies,)),
            pltpu.SemaphoreType.DMA((8,)),
        ],
        compiler_params=pltpu.CompilerParams(
            collective_id=0, has_side_effects=True, vmem_limit_bytes=48 * 1024 * 1024
        ),
    )(
        *(
            pltpu.with_memory_space_constraint(a, pltpu.HBM)
            for a in (
                intersection,
                cotangent[0, 0, 0],
                metric[0, 0, 0],
                volume_ops[0],
                face_ops[0],
                land_mask[0],
            )
        )
    )
    return out[None, None, None]


def solution(mesh):
    in_specs = (
        P("comp", "gx", "gy", None, None),
        P("comp", "gx", "gy", None, None),
        P("comp", None, None),
        P("comp", None, None, None),
        P("gx", "gy", None),
        P(),
    )
    out_specs = P("comp", "gx", "gy", None, None)
    return jax.shard_map(body, mesh=mesh, in_specs=in_specs, out_specs=out_specs, check_vma=False)
```
